256 devices in a mesh: head: 8 (over y, x_hi), inner: 4 (over x_lo, core), outer: 8 (over z).
Axes of the slice: x: 4 (x_hi: 2, x_lo: 2; x = x_hi * 2 + x_lo), y: 4, z: 8, core: 2. Of those that a mesh axis runs over, the one named last changes fastest.
Arguments:
- queries: bfloat16 [16384, 4096], P(('head', 'inner', 'outer')), may hold values from -6 to 6
- key_rows: bfloat16 [16384, 1024], P(('head', 'inner', 'outer')), may hold values from -6 to 6
- value_rows: bfloat16 [16384, 1024], P(('head', 'inner', 'outer')), may hold values from -6 to 6
- outputs: bfloat16 [16384, 4096], P(('head', 'inner', 'outer')), may hold values from -1.5 to 1.5
- out_grads: bfloat16 [16384, 4096], P(('head', 'inner', 'outer')), may hold values from -24 to 24
- log_norms: float32 [32, 16384], P(None, ('head', 'inner', 'outer')), as said below
Outputs:
- query_grads: bfloat16 [16384, 4096], P(('head', 'inner', 'outer'))
- key_grads: bfloat16 [16384, 1024], P(('head', 'inner', 'outer'))
- value_grads: bfloat16 [16384, 1024], P(('head', 'inner', 'outer'))
The draws below stay inside these ranges and needn't reach their ends.
Inputs may be any that keep to these rules, and one draw needn't show every extreme that they name: `log_norms`: within 1 of 0.5 * ln(p + 1) + 1.5, where p = (row index) % 2048 is the row's index in its sequence.
All inputs are finite; a program needn't handle non-finite values.
Results may differ from the reference program's by a relative error of at most 0.0051.
Values may be sent and summed in bfloat16 or wider, within the bound.
A program may use at most 128 MiB of HBM per device.

```python
import math
import jax
import jax.numpy as jnp
from jax import lax

HQ = 32
HK = 8
HD = 128
TOK_DEV = 64
SEQ = 2048
SEQS = 8
ROWS = 16384
N_INNER = 4
N_OUTER = 8


def draw_log_norms(key, part):
    key = jax.random.fold_in(key, 7)
    positions = (jnp.arange(ROWS, dtype=jnp.int32) % SEQ).astype(jnp.float32)
    centre = 0.5 * jnp.log(positions + 1.0) + 1.5
    jitter = jax.random.uniform(key, (HQ, ROWS), jnp.float32, -0.5, 0.5)
    return (centre[None, :] + jitter).astype(jnp.float32)


def level_of(stream_key, dims, shards, smallest, high):
    factor_of = 1.0
    for axis_at, shards_of in shards:
        steps = jax.random.uniform(jax.random.fold_in(jax.random.fold_in(stream_key, 6), axis_at), (shards_of,), jnp.float32, smallest / len(shards), high / len(shards))
        factor_of = factor_of * jnp.repeat(jnp.exp(steps), dims[axis_at] // shards_of).reshape((-1,) + (1,) * (len(dims) - 1 - axis_at))
    return factor_of


def normal_values(key, extent, deviation, reach, split=(), kind=jnp.bfloat16):
    result = deviation * jax.random.normal(key, extent, jnp.float32)
    if split:
        result = result * level_of(key, extent, split, -0.22, 0.18)
    return jnp.clip(result, -reach, reach).astype(kind)


def setup_inputs(seed: int = 0) -> dict:
    key_list = jax.random.split(jax.random.key(seed), 7)
    queries = normal_values(key_list[0], (ROWS, HQ * HD), 1.0, 6.0, ((0, 256),))
    key_rows = normal_values(key_list[1], (ROWS, HK * HD), 1.0, 6.0, ((0, 256),))
    value_rows = normal_values(key_list[2], (ROWS, HK * HD), 1.0, 6.0, ((0, 256),))
    outputs = normal_values(key_list[3], (ROWS, HQ * HD), 0.25, 1.5, ((0, 256),))
    out_grads = normal_values(key_list[4], (ROWS, HQ * HD), 4.0, 24.0, ((0, 256),))
    log_norms = draw_log_norms(jax.random.fold_in(key_list[6], 71), 0)
    return dict(queries=queries, key_rows=key_rows, value_rows=value_rows, outputs=outputs, out_grads=out_grads, log_norms=log_norms)


def token_positions():
    ctx_count = N_INNER * N_OUTER
    half = TOK_DEV // 2
    index = jnp.arange(SEQ, dtype=jnp.int32)
    device = index // TOK_DEV
    within = index % TOK_DEV
    early = device * half + within
    late = (2 * ctx_count - 1 - device) * half + within - half
    return jnp.where(within < half, early, late).astype(jnp.int32)


def group_grads(arrays):
    q_group, k_group, v_group, do_group, delta_group, lse_group = arrays
    score_scale = HD ** -0.5
    block = math.gcd(SEQ, 512)
    columns = token_positions()
    key_wide = k_group.astype(jnp.float32)
    value_wide = v_group.astype(jnp.float32)
    highest = lax.Precision.HIGHEST

    def one_block(carry, index):
        dk_total, dv_total = carry
        start = (index * block).astype(jnp.int32)
        q_block = lax.dynamic_slice_in_dim(q_group, start, block, 0).astype(jnp.float32)
        do_block = lax.dynamic_slice_in_dim(do_group, start, block, 0).astype(jnp.float32)
        delta_block = lax.dynamic_slice_in_dim(delta_group, start, block, 0)
        lse_block = lax.dynamic_slice_in_dim(lse_group, start, block, 1)
        row_ids = lax.dynamic_slice_in_dim(columns, start, block, 0)
        scores = jnp.einsum("tgd,ud->gtu", q_block, key_wide, precision=highest) * score_scale
        allowed = columns[None, :] <= row_ids[:, None]
        weights = jnp.where(allowed[None], jnp.exp(scores - lse_block[:, :, None]), 0.0)
        weights_low = lax.optimization_barrier(weights.astype(jnp.bfloat16)).astype(jnp.float32)
        dv_part = jnp.einsum("gtu,tgd->ud", weights_low, do_block, precision=highest)
        dweights = jnp.einsum("tgd,ud->gtu", do_block, value_wide, precision=highest)
        dscores = weights * (dweights - jnp.transpose(delta_block)[:, :, None]) * score_scale
        dscores_low = lax.optimization_barrier(dscores.astype(jnp.bfloat16)).astype(jnp.float32)
        dq_block = jnp.einsum("gtu,ud->tgd", dscores_low, key_wide, precision=highest).astype(jnp.bfloat16)
        dk_part = jnp.einsum("gtu,tgd->ud", dscores_low, q_block, precision=highest)
        return (dk_total + dk_part, dv_total + dv_part), dq_block

    zero_rows = jnp.zeros((SEQ, HD), jnp.float32)
    sums, dq_blocks = lax.scan(one_block, (zero_rows, zero_rows), jnp.arange(SEQ // block, dtype=jnp.int32))
    dq_group = dq_blocks.reshape(SEQ, HQ // HK, HD)
    return dq_group, sums[0].astype(jnp.bfloat16), sums[1].astype(jnp.bfloat16)


def one_sequence(arrays):
    queries, key_rows, value_rows, outputs, out_grads, log_norms = arrays
    group_size = HQ // HK
    q_heads = jnp.transpose(queries.reshape(SEQ, HK, group_size, HD), (1, 0, 2, 3))
    k_heads = jnp.transpose(key_rows.reshape(SEQ, HK, HD), (1, 0, 2))
    v_heads = jnp.transpose(value_rows.reshape(SEQ, HK, HD), (1, 0, 2))
    do_heads = jnp.transpose(out_grads.reshape(SEQ, HK, group_size, HD), (1, 0, 2, 3))
    out_heads = jnp.transpose(outputs.reshape(SEQ, HK, group_size, HD), (1, 0, 2, 3))
    delta_heads = jnp.sum(do_heads.astype(jnp.float32) * out_heads.astype(jnp.float32), axis=3)
    lse_heads = log_norms.reshape(HK, group_size, SEQ)
    dq_all, dk_all, dv_all = lax.map(group_grads, (q_heads, k_heads, v_heads, do_heads, delta_heads, lse_heads))
    query_grads = jnp.transpose(dq_all, (1, 0, 2, 3)).reshape(SEQ, HQ * HD)
    key_grads = jnp.transpose(dk_all, (1, 0, 2)).reshape(SEQ, HK * HD)
    value_grads = jnp.transpose(dv_all, (1, 0, 2)).reshape(SEQ, HK * HD)
    return (query_grads, key_grads, value_grads)


def reference(queries, key_rows, value_rows, outputs, out_grads, log_norms):
    split_q = queries.reshape(SEQS, SEQ, HQ * HD)
    split_k = key_rows.reshape(SEQS, SEQ, HK * HD)
    split_v = value_rows.reshape(SEQS, SEQ, HK * HD)
    split_out = outputs.reshape(SEQS, SEQ, HQ * HD)
    split_do = out_grads.reshape(SEQS, SEQ, HQ * HD)
    split_lse = jnp.transpose(log_norms.reshape(HQ, SEQS, SEQ), (1, 0, 2))
    dq_all, dk_all, dv_all = lax.map(one_sequence, (split_q, split_k, split_v, split_out, split_do, split_lse))
    return (dq_all.reshape(ROWS, HQ * HD), dk_all.reshape(ROWS, HK * HD), dv_all.reshape(ROWS, HK * HD))
```

```python
import functools

import jax
import jax.numpy as jnp
from jax import lax
from jax.experimental import pallas as pl
from jax.experimental.pallas import tpu as pltpu
from jax.sharding import PartitionSpec as P

HQ = 32
HK = 8
HD = 128
GROUP = HQ // HK
TOK = 64
HALF = TOK // 2
NZ = 8
NI = 4
GCOLS = GROUP * HD
LOG2E = 1.4426950408889634
SCALE = HD ** -0.5
MESH = pl.DeviceIdType.MESH
F32 = jnp.float32
BF16 = jnp.bfloat16
ORDER = (1, 7, 2, 6, 3, 5, 4)
GROUPS = ((0, 1), (7, 2), (6, 3), (5, 4))


def dot(a, b, dims):
    return lax.dot_general(a, b, (dims, ((), ())), preferred_element_type=F32)


def kernel(
    q_hbm, k_hbm, v_hbm, o_hbm, do_hbm, lse_hbm,
    dq_out, dk_out, dv_out,
    o_in, do_in, lse_in, lse_wide, aux_send, aux, kv, qb, dob,
    k_t, q_rows, do_rows, dq_acc, dq_stage, dk_acc, dv_acc,
    part_send, part_recv, kv_stage,
    local_sem, kv_s, kv_r, aux_s, aux_r, q_s, q_r, do_s, do_r,
    relay_s, relay_r, dq_s, dq_r, part_s, part_r, out_s, out_r,
):
    me = lax.axis_index("inner")
    z = lax.axis_index("outer")

    def ring(step):
        return lax.rem(z + step, NZ)

    def at_ring(step):
        return {"outer": ring(step)}

    def at_plane(x):
        return {"inner": me ^ x}

    def q_cols(index):
        return pl.ds(pl.multiple_of(index * GCOLS, GCOLS), GCOLS)

    def k_cols(index):
        return pl.ds(pl.multiple_of(index * HD, HD), HD)

    barrier = pltpu.get_barrier_semaphore()
    for step in range(1, NZ):
        pl.semaphore_signal(barrier, inc=1, device_id=at_ring(step), device_id_type=MESH)
    for x in range(1, NI):
        pl.semaphore_signal(barrier, inc=1, device_id=at_plane(x), device_id_type=MESH)

    locals_ = [
        pltpu.make_async_copy(k_hbm.at[:, k_cols(z)], kv.at[me, 0, 0], local_sem.at[0]),
        pltpu.make_async_copy(v_hbm.at[:, k_cols(z)], kv.at[me, 0, 1], local_sem.at[1]),
        pltpu.make_async_copy(q_hbm.at[:, q_cols(z)], qb.at[0], local_sem.at[2]),
        pltpu.make_async_copy(do_hbm.at[:, q_cols(z)], dob.at[0], local_sem.at[3]),
        pltpu.make_async_copy(o_hbm, o_in, local_sem.at[4]),
        pltpu.make_async_copy(do_hbm, do_in, local_sem.at[5]),
        pltpu.make_async_copy(lse_hbm, lse_in, local_sem.at[6]),
    ]
    for copy in locals_:
        copy.start()
    pl.semaphore_wait(barrier, NZ - 1 + NI - 1)

    def remote(src, dst, send, recv, where):
        return pltpu.make_async_remote_copy(
            src_ref=src, dst_ref=dst, send_sem=send, recv_sem=recv,
            device_id=where, device_id_type=MESH,
        )

    sends = []
    k_in = {}
    q_in = {}
    for step in ORDER:
        slot = NZ - step
        there = ring(step)
        pair = [
            remote(ref.at[:, k_cols(there)], kv.at[me, slot, n], kv_s.at[n, slot],
                   kv_r.at[n, slot], at_ring(step))
            for n, ref in enumerate((k_hbm, v_hbm))
        ]
        for copy in pair:
            copy.start()
        sends += pair
        k_in[slot] = pair

    for n in (4, 5, 6):
        locals_[n].wait()
    lse_wide[...] = jnp.zeros_like(lse_wide)
    lse_wide[:, 0:TOK] = lse_in[...]
    norms = lse_wide[...] * LOG2E
    rows = lax.broadcasted_iota(jnp.int32, norms.shape, 0)
    lanes = lax.broadcasted_iota(jnp.int32, norms.shape, 1)
    for late in range(2):
        picked = jnp.zeros_like(norms)
        for h in range(GROUP):
            moved = norms
            shift = (h - late) * HALF % HD
            if shift:
                moved = pltpu.roll(norms, shift, 1)
            here = (rows % GROUP == h) & (lanes // HALF == h)
            picked = jnp.where(here, moved, picked)
        total = picked
        for h in range(1, GROUP):
            total = total + pltpu.roll(picked, HQ - h, 0)
        for g in range(HK):
            aux_send[g, late:late + 1, :] = total[GROUP * g:GROUP * g + 1, :]
    ones = jnp.ones((8, HD), BF16)
    for g in range(HK):
        blocks = []
        for late in range(2):
            for h in range(GROUP):
                part = (slice(late * HALF, (late + 1) * HALF),
                        slice((g * GROUP + h) * HD, (g * GROUP + h + 1) * HD))
                blocks.append(do_in[part].astype(F32) * o_in[part].astype(F32))
        product = jnp.concatenate(blocks, axis=0)
        high = product.astype(BF16)
        low = (product - high.astype(F32)).astype(BF16)
        sums = dot(ones, high, ((1,), (1,))) + dot(ones, low, ((1,), (1,)))
        aux_send[g, 2:3, :] = sums[0:1, 0:HD]
        aux_send[g, 3:4, :] = sums[0:1, HD:2 * HD]
    aux[0] = aux_send[z]

    for step in ORDER:
        slot = NZ - step
        there = ring(step)
        trio = [
            remote(aux_send.at[there], aux.at[slot], aux_s.at[slot], aux_r.at[slot], at_ring(step)),
            remote(q_hbm.at[:, q_cols(there)], qb.at[slot], q_s.at[slot], q_r.at[slot], at_ring(step)),
            remote(do_hbm.at[:, q_cols(there)], dob.at[slot], do_s.at[slot], do_r.at[slot], at_ring(step)),
        ]
        for copy in trio:
            copy.start()
        sends += trio
        q_in[slot] = trio

    relays = {}
    for slot in (0,) + tuple(NZ - step for step in ORDER):
        if slot == 0:
            locals_[0].wait()
            locals_[1].wait()
        else:
            for copy in k_in[slot]:
                copy.wait_recv()
        for x in (3, 2, 1):
            copy = remote(kv.at[me, slot], kv.at[me, slot], relay_s.at[x - 1, slot],
                          relay_r.at[x - 1, slot], at_plane(x))
            copy.start()
            sends.append(copy)
            relays[x, slot] = copy

    def transpose_keys(owner):
        for late in range(2):
            rows_ = kv[owner, :, 0, late * HALF:(late + 1) * HALF, :].reshape(NZ * HALF, HD)
            k_t[late, owner] = rows_.T

    transpose_keys(me)
    for x in (1, 2, 3):
        for slot in range(NZ):
            pltpu.make_async_remote_copy(
                src_ref=kv.at[me ^ x, slot], dst_ref=kv.at[me ^ x, slot],
                send_sem=relay_s.at[x - 1, slot], recv_sem=relay_r.at[x - 1, slot],
                device_id=at_plane(x), device_id_type=MESH,
            ).wait_recv()
        transpose_keys(me ^ x)

    dk_acc[...] = jnp.zeros_like(dk_acc)
    dv_acc[...] = jnp.zeros_like(dv_acc)
    dq_sends = []

    for turn, slots in enumerate(GROUPS):
        last = turn == len(GROUPS) - 1
        width = len(slots) * GROUP * HALF
        for n, slot in enumerate(slots):
            if slot == 0:
                locals_[2].wait()
                locals_[3].wait()
            else:
                for copy in q_in[slot]:
                    copy.wait_recv()
            for late in range(2):
                for h in range(GROUP):
                    to = slice((n * GROUP + h) * HALF, (n * GROUP + h + 1) * HALF)
                    tok = slice(late * HALF, (late + 1) * HALF)
                    col = slice(h * HD, (h + 1) * HD)
                    q_rows[late, to, :] = qb[slot, tok, col]
                    do_rows[late, to, :] = dob[slot, tok, col]
        dq_acc[...] = jnp.zeros_like(dq_acc)

        def tile(q_late, k_late, owner, diagonal):
            tok = pl.ds(pl.multiple_of(k_late * HALF, HALF), HALF)
            keys = kv[owner, :, 0, tok, :].reshape(NZ * HALF, HD)
            values = kv[owner, :, 1, tok, :].reshape(NZ * HALF, HD)
            q_part = q_rows[q_late, 0:width]
            do_part = do_rows[q_late, 0:width]
            norm = jnp.concatenate([aux[slot, pl.ds(q_late, 1), :] for slot in slots], axis=1)
            delta = jnp.concatenate([aux[slot, pl.ds(q_late + 2, 1), :] for slot in slots], axis=1)
            scores = dot(keys, q_part, ((1,), (1,)))
            weights = jnp.exp2(scores * (SCALE * LOG2E) - norm)
            if diagonal:
                key_row = lax.broadcasted_iota(jnp.int32, (NZ * HALF, 1), 0)
                q_lane = lax.broadcasted_iota(jnp.int32, (1, width), 1)
                key_z = (z + key_row // HALF) % NZ
                q_slot = jnp.full((1, width), slots[0], jnp.int32)
                for n, slot in enumerate(slots):
                    q_slot = jnp.where(q_lane // (GROUP * HALF) == n, slot, q_slot)
                q_z = (z + q_slot) % NZ
                sign = 1 if diagonal == 1 else -1
                key_at = sign * key_z * HALF + key_row % HALF
                q_at = sign * q_z * HALF + q_lane % HALF
                weights = jnp.where(key_at <= q_at, weights, 0.0)
            weights_low = weights.astype(BF16)
            dv_acc[owner, :, tok, :] += dot(weights_low, do_part, ((1,), (0,))).reshape(NZ, HALF, HD)
            dweights = dot(values, do_part, ((1,), (1,)))
            dscores = (weights * (dweights - delta)).astype(BF16)
            dk_acc[owner, :, tok, :] += dot(dscores, q_part, ((1,), (0,))).reshape(NZ, HALF, HD)
            dq_acc[q_late, :, 0:width] += dot(k_t[k_late, owner], dscores, ((1,), (0,)))

        for x in (3, 2, 1):
            owner = me ^ x
            tile(1, 0, owner, 0)
            above = (owner > me).astype(jnp.int32)
            tile(above, above, owner, 0)
            if last:
                part_send[x - 1, :, 0] = dk_acc[owner].astype(BF16)
                part_send[x - 1, :, 1] = dv_acc[owner].astype(BF16)
                copy = remote(part_send.at[x - 1], part_recv.at[x - 1], part_s.at[x - 1],
                              part_r.at[x - 1], at_plane(x))
                copy.start()
                sends.append(copy)
                relays["part", x] = copy
        tile(1, 0, me, 0)
        tile(0, 0, me, 1)
        tile(1, 1, me, 2)

        for late in range(2):
            back = (dq_acc[late, :, 0:width] * SCALE).T.astype(BF16)
            for n, slot in enumerate(slots):
                for h in range(GROUP):
                    rows_ = slice((n * GROUP + h) * HALF, (n * GROUP + h + 1) * HALF)
                    dq_stage[slot, late * HALF:(late + 1) * HALF, h * HD:(h + 1) * HD] = back[rows_]
        for slot in slots:
            if slot == 0:
                copy = pltpu.make_async_copy(dq_stage.at[0], dq_out.at[:, q_cols(z)], dq_s.at[0])
            else:
                copy = remote(dq_stage.at[slot], dq_out.at[:, q_cols(z)], dq_s.at[slot],
                              dq_r.at[slot], at_ring(slot))
            copy.start()
            dq_sends.append((slot, copy))

    for x in (1, 2, 3):
        relays["part", x].wait_recv()
    kv_out = []
    for slot in (1, 7, 2, 6, 3, 5, 4, 0):
        for n, (acc, factor) in enumerate(((dk_acc, SCALE), (dv_acc, 1.0))):
            total = acc[me, slot]
            for x in range(1, NI):
                total = total + part_recv[x - 1, slot, n].astype(F32)
            if factor != 1.0:
                total = total * factor
            kv_stage[slot, n] = total.astype(BF16)
            out = (dk_out, dv_out)[n]
            if slot == 0:
                copy = pltpu.make_async_copy(kv_stage.at[0, n], out.at[:, k_cols(z)], out_s.at[n, 0])
            else:
                copy = remote(kv_stage.at[slot, n], out.at[:, k_cols(z)], out_s.at[n, slot],
                              out_r.at[n, slot], at_ring(slot))
            copy.start()
            kv_out.append((slot, n, copy))

    for copy in sends:
        copy.wait_send()
    for slot, copy in dq_sends:
        if slot == 0:
            copy.wait()
        else:
            copy.wait_send()
            came = q_cols(ring(NZ - slot))
            remote(dq_stage.at[slot], dq_out.at[:, came], dq_s.at[slot], dq_r.at[slot],
                   at_ring(slot)).wait_recv()
    for slot, n, copy in kv_out:
        if slot == 0:
            copy.wait()
        else:
            copy.wait_send()
            came = k_cols(ring(NZ - slot))
            out = (dk_out, dv_out)[n]
            remote(kv_stage.at[slot, n], out.at[:, came], out_s.at[n, slot], out_r.at[n, slot],
                   at_ring(slot)).wait_recv()


def on_device(queries, key_rows, value_rows, outputs, out_grads, log_norms):
    dma = pltpu.SemaphoreType.DMA
    width = max(len(slots) for slots in GROUPS) * GROUP * HALF
    return pl.pallas_call(
        kernel,
        out_shape=(
            jax.ShapeDtypeStruct((TOK, HQ * HD), BF16),
            jax.ShapeDtypeStruct((TOK, HK * HD), BF16),
            jax.ShapeDtypeStruct((TOK, HK * HD), BF16),
        ),
        in_specs=[pl.BlockSpec(memory_space=pl.ANY)] * 6,
        out_specs=(pl.BlockSpec(memory_space=pl.ANY),) * 3,
        scratch_shapes=[
            pltpu.VMEM((TOK, HQ * HD), BF16),
            pltpu.VMEM((TOK, HQ * HD), BF16),
            pltpu.VMEM((HQ, TOK), F32),
            pltpu.VMEM((HQ, HD), F32),
            pltpu.VMEM((NZ, 8, HD), F32),
            pltpu.VMEM((NZ, 8, HD), F32),
            pltpu.VMEM((NI, NZ, 2, TOK, HD), BF16),
            pltpu.VMEM((NZ, TOK, GCOLS), BF16),
            pltpu.VMEM((NZ, TOK, GCOLS), BF16),
            pltpu.VMEM((2, NI, HD, NZ * HALF), BF16),
            pltpu.VMEM((2, width, HD), BF16),
            pltpu.VMEM((2, width, HD), BF16),
            pltpu.VMEM((2, HD, width), F32),
            pltpu.VMEM((NZ, TOK, GCOLS), BF16),
            pltpu.VMEM((NI, NZ, TOK, HD), F32),
            pltpu.VMEM((NI, NZ, TOK, HD), F32),
            pltpu.VMEM((NI - 1, NZ, 2, TOK, HD), BF16),
            pltpu.VMEM((NI - 1, NZ, 2, TOK, HD), BF16),
            pltpu.VMEM((NZ, 2, TOK, HD), BF16),
            dma((7,)),
            dma((2, NZ)), dma((2, NZ)),
            dma((NZ,)), dma((NZ,)),
            dma((NZ,)), dma((NZ,)),
            dma((NZ,)), dma((NZ,)),
            dma((NI - 1, NZ)), dma((NI - 1, NZ)),
            dma((NZ,)), dma((NZ,)),
            dma((NI - 1,)), dma((NI - 1,)),
            dma((2, NZ)), dma((2, NZ)),
        ],
        compiler_params=pltpu.CompilerParams(
            collective_id=0, has_side_effects=True, vmem_limit_bytes=48 << 20
        ),
    )(queries, key_rows, value_rows, outputs, out_grads, log_norms)


def solution(mesh):
    rows = P(("head", "inner", "outer"), None)
    return jax.shard_map(
        on_device,
        mesh=mesh,
        in_specs=(rows,) * 5 + (P(None, ("head", "inner", "outer")),),
        out_specs=(rows,) * 3,
        check_vma=False,
    )
```

```python
import functools

import jax
import jax.numpy as jnp
from jax import lax
from jax.experimental import pallas as pl
from jax.experimental.pallas import tpu as pltpu
from jax.sharding import PartitionSpec as P

HQ = 32
HK = 8
HD = 128
GROUP = HQ // HK
TOK = 64
HALF = TOK // 2
NZ = 8
NI = 4
GCOLS = GROUP * HD
LOG2E = 1.4426950408889634
SCALE = HD ** -0.5
MESH = pl.DeviceIdType.MESH
F32 = jnp.float32
BF16 = jnp.bfloat16
ORDER = (1, 7, 2, 6, 3, 5, 4)
GROUPS = ((0, 1), (7, 2), (6, 3), (5, 4))


def dot(a, b, dims):
    return lax.dot_general(a, b, (dims, ((), ())), preferred_element_type=F32)


def kernel(
    q_hbm, k_hbm, v_hbm, o_hbm, do_hbm, lse_hbm,
    dq_out, dk_out, dv_out,
    o_in, do_in, lse_in, lse_wide, aux_send, aux, kv, qb, dob,
    k_t, q_rows, do_rows, dq_acc, dq_stage, dk_acc, dv_acc,
    part_send, part_recv, kv_stage,
    local_sem, kv_s, kv_r, aux_s, aux_r, q_s, q_r, do_s, do_r,
    relay_s, relay_r, dq_s, dq_r, part_s, part_r, out_s, out_r,
):
    me = lax.axis_index("inner")
    z = lax.axis_index("outer")

    def ring(step):
        return lax.rem(z + step, NZ)

    def at_ring(step):
        return {"outer": ring(step)}

    def at_plane(x):
        return {"inner": me ^ x}

    def q_cols(index):
        return pl.ds(pl.multiple_of(index * GCOLS, GCOLS), GCOLS)

    def k_cols(index):
        return pl.ds(pl.multiple_of(index * HD, HD), HD)

    barrier = pltpu.get_barrier_semaphore()
    for step in range(1, NZ):
        pl.semaphore_signal(barrier, inc=1, device_id=at_ring(step), device_id_type=MESH)
    for x in range(1, NI):
        pl.semaphore_signal(barrier, inc=1, device_id=at_plane(x), device_id_type=MESH)

    locals_ = [
        pltpu.make_async_copy(k_hbm.at[:, k_cols(z)], kv.at[me, 0, 0], local_sem.at[0]),
        pltpu.make_async_copy(v_hbm.at[:, k_cols(z)], kv.at[me, 0, 1], local_sem.at[1]),
        pltpu.make_async_copy(q_hbm.at[:, q_cols(z)], qb.at[0], local_sem.at[2]),
        pltpu.make_async_copy(do_hbm.at[:, q_cols(z)], dob.at[0], local_sem.at[3]),
        pltpu.make_async_copy(o_hbm, o_in, local_sem.at[4]),
        pltpu.make_async_copy(do_hbm, do_in, local_sem.at[5]),
        pltpu.make_async_copy(lse_hbm, lse_in, local_sem.at[6]),
    ]
    for copy in locals_:
        copy.start()
    pl.semaphore_wait(barrier, NZ - 1 + NI - 1)

    def remote(src, dst, send, recv, where):
        return pltpu.make_async_remote_copy(
            src_ref=src, dst_ref=dst, send_sem=send, recv_sem=recv,
            device_id=where, device_id_type=MESH,
        )

    sends = []
    k_in = {}
    q_in = {}
    for step in ORDER:
        slot = NZ - step
        there = ring(step)
        pair = [
            remote(ref.at[:, k_cols(there)], kv.at[me, slot, n], kv_s.at[n, slot],
                   kv_r.at[n, slot], at_ring(step))
            for n, ref in enumerate((k_hbm, v_hbm))
        ]
        for copy in pair:
            copy.start()
        sends += pair
        k_in[slot] = pair

    for n in (4, 5, 6):
        locals_[n].wait()
    lse_wide[...] = jnp.zeros_like(lse_wide)
    lse_wide[:, 0:TOK] = lse_in[...]
    norms = lse_wide[...] * LOG2E
    rows = lax.broadcasted_iota(jnp.int32, norms.shape, 0)
    lanes = lax.broadcasted_iota(jnp.int32, norms.shape, 1)
    for late in range(2):
        picked = jnp.zeros_like(norms)
        for h in range(GROUP):
            moved = norms
            shift = (h - late) * HALF % HD
            if shift:
                moved = pltpu.roll(norms, shift, 1)
            here = (rows % GROUP == h) & (lanes // HALF == h)
            picked = jnp.where(here, moved, picked)
        total = picked
        for h in range(1, GROUP):
            total = total + pltpu.roll(picked, HQ - h, 0)
        for g in range(HK):
            aux_send[g, late:late + 1, :] = total[GROUP * g:GROUP * g + 1, :]
    ones = jnp.ones((8, HD), BF16)
    for g in range(HK):
        blocks = []
        for late in range(2):
            for h in range(GROUP):
                part = (slice(late * HALF, (late + 1) * HALF),
                        slice((g * GROUP + h) * HD, (g * GROUP + h + 1) * HD))
                blocks.append(do_in[part].astype(F32) * o_in[part].astype(F32))
        product = jnp.concatenate(blocks, axis=0)
        high = product.astype(BF16)
        low = (product - high.astype(F32)).astype(BF16)
        sums = dot(ones, high, ((1,), (1,))) + dot(ones, low, ((1,), (1,)))
        aux_send[g, 2:3, :] = sums[0:1, 0:HD]
        aux_send[g, 3:4, :] = sums[0:1, HD:2 * HD]
    aux[0] = aux_send[z]

    for step in ORDER:
        slot = NZ - step
        there = ring(step)
        trio = [
            remote(aux_send.at[there], aux.at[slot], aux_s.at[slot], aux_r.at[slot], at_ring(step)),
            remote(q_hbm.at[:, q_cols(there)], qb.at[slot], q_s.at[slot], q_r.at[slot], at_ring(step)),
            remote(do_hbm.at[:, q_cols(there)], dob.at[slot], do_s.at[slot], do_r.at[slot], at_ring(step)),
        ]
        for copy in trio:
            copy.start()
        sends += trio
        q_in[slot] = trio

    relays = {}
    for slot in (0,) + tuple(NZ - step for step in ORDER):
        if slot == 0:
            locals_[0].wait()
            locals_[1].wait()
        else:
            for copy in k_in[slot]:
                copy.wait_recv()
        for x in (3, 2, 1):
            copy = remote(kv.at[me, slot], kv.at[me, slot], relay_s.at[x - 1, slot],
                          relay_r.at[x - 1, slot], at_plane(x))
            copy.start()
            sends.append(copy)
            relays[x, slot] = copy

    def transpose_keys(owner):
        for late in range(2):
            rows_ = kv[owner, :, 0, late * HALF:(late + 1) * HALF, :].reshape(NZ * HALF, HD)
            k_t[late, owner] = rows_.T

    transpose_keys(me)
    for x in (1, 2, 3):
        for slot in range(NZ):
            pltpu.make_async_remote_copy(
                src_ref=kv.at[me ^ x, slot], dst_ref=kv.at[me ^ x, slot],
                send_sem=relay_s.at[x - 1, slot], recv_sem=relay_r.at[x - 1, slot],
                device_id=at_plane(x), device_id_type=MESH,
            ).wait_recv()
        transpose_keys(me ^ x)

    dk_acc[...] = jnp.zeros_like(dk_acc)
    dv_acc[...] = jnp.zeros_like(dv_acc)
    dq_sends = []

    for turn, slots in enumerate(GROUPS):
        last = turn == len(GROUPS) - 1
        width = len(slots) * GROUP * HALF
        for n, slot in enumerate(slots):
            if slot == 0:
                locals_[2].wait()
                locals_[3].wait()
            else:
                for copy in q_in[slot]:
                    copy.wait_recv()
            for late in range(2):
                for h in range(GROUP):
                    to = slice((n * GROUP + h) * HALF, (n * GROUP + h + 1) * HALF)
                    tok = slice(late * HALF, (late + 1) * HALF)
                    col = slice(h * HD, (h + 1) * HD)
                    q_rows[late, to, :] = qb[slot, tok, col]
                    do_rows[late, to, :] = dob[slot, tok, col]
        dq_acc[...] = jnp.zeros_like(dq_acc)

        def tile(q_late, k_late, owner, diagonal):
            tok = pl.ds(pl.multiple_of(k_late * HALF, HALF), HALF)
            keys = kv[owner, :, 0, tok, :].reshape(NZ * HALF, HD)
            values = kv[owner, :, 1, tok, :].reshape(NZ * HALF, HD)
            q_part = q_rows[q_late, 0:width]
            do_part = do_rows[q_late, 0:width]
            norm = jnp.concatenate([aux[slot, pl.ds(q_late, 1), :] for slot in slots], axis=1)
            delta = jnp.concatenate([aux[slot, pl.ds(q_late + 2, 1), :] for slot in slots], axis=1)
            scores = dot(keys, q_part, ((1,), (1,)))
            weights = jnp.exp2(scores * (SCALE * LOG2E) - norm)
            if diagonal:
                key_row = lax.broadcasted_iota(jnp.int32, (NZ * HALF, 1), 0)
                q_lane = lax.broadcasted_iota(jnp.int32, (1, width), 1)
                key_z = (z + key_row // HALF) % NZ
                q_slot = jnp.full((1, width), slots[0], jnp.int32)
                for n, slot in enumerate(slots):
                    q_slot = jnp.where(q_lane // (GROUP * HALF) == n, slot, q_slot)
                q_z = (z + q_slot) % NZ
                sign = 1 if diagonal == 1 else -1
                key_at = sign * key_z * HALF + key_row % HALF
                q_at = sign * q_z * HALF + q_lane % HALF
                weights = jnp.where(key_at <= q_at, weights, 0.0)
            weights_low = weights.astype(BF16)
            dv_acc[owner, :, tok, :] += dot(weights_low, do_part, ((1,), (0,))).reshape(NZ, HALF, HD)
            dweights = dot(values, do_part, ((1,), (1,)))
            dscores = (weights * (dweights - delta)).astype(BF16)
            dk_acc[owner, :, tok, :] += dot(dscores, q_part, ((1,), (0,))).reshape(NZ, HALF, HD)
            dq_acc[q_late, :, 0:width] += dot(k_t[k_late, owner], dscores, ((1,), (0,)))

        for x in (3, 2, 1):
            owner = me ^ x
            tile(1, 0, owner, 0)
            above = (owner > me).astype(jnp.int32)
            tile(above, above, owner, 0)
            if last:
                part_send[x - 1, :, 0] = dk_acc[owner].astype(BF16)
                part_send[x - 1, :, 1] = dv_acc[owner].astype(BF16)
                copy = remote(part_send.at[x - 1], part_recv.at[x - 1], part_s.at[x - 1],
                              part_r.at[x - 1], at_plane(x))
                copy.start()
                sends.append(copy)
                relays["part", x] = copy
        tile(1, 0, me, 0)
        tile(0, 0, me, 1)
        tile(1, 1, me, 2)

        for late in range(2):
            back = (dq_acc[late, :, 0:width] * SCALE).T.astype(BF16)
            for n, slot in enumerate(slots):
                for h in range(GROUP):
                    rows_ = slice((n * GROUP + h) * HALF, (n * GROUP + h + 1) * HALF)
                    dq_stage[slot, late * HALF:(late + 1) * HALF, h * HD:(h + 1) * HD] = back[rows_]
        for slot in slots:
            if slot == 0:
                copy = pltpu.make_async_copy(dq_stage.at[0], dq_out.at[:, q_cols(z)], dq_s.at[0])
            else:
                copy = remote(dq_stage.at[slot], dq_out.at[:, q_cols(z)], dq_s.at[slot],
                              dq_r.at[slot], at_ring(slot))
            copy.start()
            dq_sends.append((slot, copy))

    for x in (1, 2, 3):
        relays["part", x].wait_recv()
    kv_out = []
    for slot in (1, 7, 2, 6, 3, 5, 4, 0):
        for n, (acc, factor) in enumerate(((dk_acc, SCALE), (dv_acc, 1.0))):
            total = acc[me, slot]
            for x in range(1, NI):
                total = total + part_recv[x - 1, slot, n].astype(F32)
            if factor != 1.0:
                total = total * factor
            kv_stage[slot, n] = total.astype(BF16)
            out = (dk_out, dv_out)[n]
            if slot == 0:
                copy = pltpu.make_async_copy(kv_stage.at[0, n], out.at[:, k_cols(z)], out_s.at[n, 0])
            else:
                copy = remote(kv_stage.at[slot, n], out.at[:, k_cols(z)], out_s.at[n, slot],
                              out_r.at[n, slot], at_ring(slot))
            copy.start()
            kv_out.append((slot, n, copy))

    for copy in sends:
        copy.wait_send()
    for slot, copy in dq_sends:
        if slot == 0:
            copy.wait()
        else:
            copy.wait_send()
            came = q_cols(ring(NZ - slot))
            remote(dq_stage.at[slot], dq_out.at[:, came], dq_s.at[slot], dq_r.at[slot],
                   at_ring(slot)).wait_recv()
    for slot, n, copy in kv_out:
        if slot == 0:
            copy.wait()
        else:
            copy.wait_send()
            came = k_cols(ring(NZ - slot))
            out = (dk_out, dv_out)[n]
            remote(kv_stage.at[slot, n], out.at[:, came], out_s.at[n, slot], out_r.at[n, slot],
                   at_ring(slot)).wait_recv()


def hand_on(*refs):
    count = len(refs) // 2
    sems = refs[-1]
    copies = [pltpu.make_async_copy(refs[n], refs[count + n], sems.at[n]) for n in range(count)]
    for copy in copies:
        copy.start()
    for copy in copies:
        copy.wait()


def on_device(queries, key_rows, value_rows, outputs, out_grads, log_norms):
    dma = pltpu.SemaphoreType.DMA
    operands = (queries, key_rows, value_rows, outputs, out_grads, log_norms)
    operands = tuple(pltpu.with_memory_space_constraint(x, pltpu.HBM) for x in operands)
    width = max(len(slots) for slots in GROUPS) * GROUP * HALF
    grads = pl.pallas_call(
        kernel,
        out_shape=(
            jax.ShapeDtypeStruct((TOK, HQ * HD), BF16),
            jax.ShapeDtypeStruct((TOK, HK * HD), BF16),
            jax.ShapeDtypeStruct((TOK, HK * HD), BF16),
        ),
        in_specs=[pl.BlockSpec(memory_space=pltpu.HBM)] * 6,
        out_specs=(pl.BlockSpec(memory_space=pl.ANY),) * 3,
        scratch_shapes=[
            pltpu.VMEM((TOK, HQ * HD), BF16),
            pltpu.VMEM((TOK, HQ * HD), BF16),
            pltpu.VMEM((HQ, TOK), F32),
            pltpu.VMEM((HQ, HD), F32),
            pltpu.VMEM((NZ, 8, HD), F32),
            pltpu.VMEM((NZ, 8, HD), F32),
            pltpu.VMEM((NI, NZ, 2, TOK, HD), BF16),
            pltpu.VMEM((NZ, TOK, GCOLS), BF16),
            pltpu.VMEM((NZ, TOK, GCOLS), BF16),
            pltpu.VMEM((2, NI, HD, NZ * HALF), BF16),
            pltpu.VMEM((2, width, HD), BF16),
            pltpu.VMEM((2, width, HD), BF16),
            pltpu.VMEM((2, HD, width), F32),
            pltpu.VMEM((NZ, TOK, GCOLS), BF16),
            pltpu.VMEM((NI, NZ, TOK, HD), F32),
            pltpu.VMEM((NI, NZ, TOK, HD), F32),
            pltpu.VMEM((NI - 1, NZ, 2, TOK, HD), BF16),
            pltpu.VMEM((NI - 1, NZ, 2, TOK, HD), BF16),
            pltpu.VMEM((NZ, 2, TOK, HD), BF16),
            dma((7,)),
            dma((2, NZ)), dma((2, NZ)),
            dma((NZ,)), dma((NZ,)),
            dma((NZ,)), dma((NZ,)),
            dma((NZ,)), dma((NZ,)),
            dma((NI - 1, NZ)), dma((NI - 1, NZ)),
            dma((NZ,)), dma((NZ,)),
            dma((NI - 1,)), dma((NI - 1,)),
            dma((2, NZ)), dma((2, NZ)),
        ],
        compiler_params=pltpu.CompilerParams(
            collective_id=0, has_side_effects=True, vmem_limit_bytes=40 << 20
        ),
    )(*operands)
    grads = tuple(pltpu.with_memory_space_constraint(g, pltpu.VMEM) for g in grads)
    return pl.pallas_call(
        hand_on,
        out_shape=tuple(jax.ShapeDtypeStruct(g.shape, g.dtype) for g in grads),
        in_specs=[pl.BlockSpec(memory_space=pltpu.VMEM)] * 3,
        out_specs=(pl.BlockSpec(memory_space=pl.ANY),) * 3,
        scratch_shapes=[dma((3,))],
    )(*grads)


def solution(mesh):
    rows = P(("head", "inner", "outer"), None)
    return jax.shard_map(
        on_device,
        mesh=mesh,
        in_specs=(rows,) * 5 + (P(None, ("head", "inner", "outer")),),
        out_specs=(rows,) * 3,
        check_vma=False,
    )
```

```python
import jax
import jax.numpy as jnp
from jax import lax
from jax.experimental import pallas as pl
from jax.experimental.pallas import tpu as pltpu
from jax.sharding import PartitionSpec as P

HQ = 32
HK = 8
HD = 128
GROUP = HQ // HK
TOK = 64
HALF = TOK // 2
NZ = 8
NI = 4
HEADS = HK // NI
QCOLS = HEADS * GROUP * HD
KEYS = NI * HALF
ROWS = NI * GROUP * HALF
LOG2E = 1.4426950408889634
SCALE = HD ** -0.5
MESH = pl.DeviceIdType.MESH
F32 = jnp.float32
BF16 = jnp.bfloat16
UP, DOWN = 1, -1


def dot(a, b, dims):
    return lax.dot_general(a, b, (dims, ((), ())), preferred_element_type=F32)


def kernel(
    q_hbm, k_hbm, v_hbm, o_hbm, do_hbm, lse_hbm,
    dq_out, sums_out,
    o_in, do_in, lse_in, lse_wide, aux_send, aux, stats, kv, qd,
    q_rows, do_rows, dq_t, dq_stage, own, part_send, part_recv, last_stage,
    local_sem, send_sem, plane_r, ring_r, part_r, rows_r, aux_r, dq_r, last_r,
):
    me = lax.axis_index("inner")
    z = lax.axis_index("outer")

    def at_ring(step):
        return {"outer": lax.rem(z + step + NZ, NZ)}

    def at_plane(x):
        return {"inner": me ^ x}

    def q_cols(index):
        return pl.ds(pl.multiple_of(index * QCOLS, QCOLS), QCOLS)

    def k_cols(index):
        return pl.ds(pl.multiple_of(index * (HEADS * HD), HEADS * HD), HEADS * HD)

    def h_cols(index, head):
        return pl.ds(pl.multiple_of(index * (HEADS * HD) + head * HD, HD), HD)

    def remote(src, dst, send, recv, where):
        return pltpu.make_async_remote_copy(
            src_ref=src, dst_ref=dst, send_sem=send, recv_sem=recv,
            device_id=where, device_id_type=MESH,
        )

    barrier = pltpu.get_barrier_semaphore()
    for step in (UP, DOWN):
        pl.semaphore_signal(barrier, inc=1, device_id=at_ring(step), device_id_type=MESH)
    for x in range(1, NI):
        pl.semaphore_signal(barrier, inc=1, device_id=at_plane(x), device_id_type=MESH)

    mine = [
        pltpu.make_async_copy(ref.at[:, k_cols(me)], kv.at[0, 0, n], local_sem.at[0])
        for n, ref in enumerate((k_hbm, v_hbm))
    ]
    rest = [
        pltpu.make_async_copy(o_hbm, o_in, local_sem.at[1]),
        pltpu.make_async_copy(do_hbm, do_in, local_sem.at[2]),
        pltpu.make_async_copy(lse_hbm, lse_in, local_sem.at[3]),
        pltpu.make_async_copy(q_hbm.at[:, q_cols(me)], qd.at[0, 0], local_sem.at[4]),
        pltpu.make_async_copy(do_hbm.at[:, q_cols(me)], qd.at[1, 0], local_sem.at[4]),
    ]
    for copy in mine + rest:
        copy.start()
    pl.semaphore_wait(barrier, 2 + NI - 1)

    def all_of(ref, send, recv):
        return remote(ref, ref, send, recv, at_plane(1))

    PLANE, RING, QD, AUX, PART, DQ = (send_sem.at[n] for n in range(6))
    LAST = send_sem.at[6:8]

    def share(x):
        for n, ref in enumerate((k_hbm, v_hbm)):
            remote(ref.at[:, k_cols(me ^ x)], kv.at[0, x, n], PLANE, plane_r.at[x - 1],
                   at_plane(x)).start()

    def pass_first(x, n, step):
        to = -step % NZ
        src = (k_hbm, v_hbm)[n].at[:, k_cols(me)] if x == 0 else kv.at[0, x, n]
        remote(src, kv.at[to, x, n], RING, ring_r.at[to - 1, x], at_ring(step)).start()

    def pass_on(slot, x, step):
        to = (slot - step) % NZ
        remote(kv.at[slot, x], kv.at[to, x], RING, ring_r.at[to - 1, x], at_ring(step)).start()

    def arrived(slot, x):
        all_of(kv.at[slot, x], RING, ring_r.at[slot - 1, x]).wait_recv()

    share(2)
    for n in range(2):
        pass_first(0, n, UP)
        pass_first(0, n, DOWN)
    share(1)
    share(3)
    for x in (2, 3, 1):
        for n, ref in enumerate((q_hbm, do_hbm)):
            remote(ref.at[:, q_cols(me ^ x)], qd.at[n, x], QD, rows_r.at[0], at_plane(x)).start()
    for x in (1, 2, 3):
        all_of(kv.at[0, x], PLANE, plane_r.at[x - 1]).wait_recv()
        for n in range(2):
            pass_first(x, n, UP)
            pass_first(x, n, DOWN)

    def flow(up_slot, down_slot, pieces=range(NI)):
        for x in pieces:
            for slot, step, far in ((up_slot, UP, 0), (down_slot, DOWN, 1)):
                arrived(slot, x)
                if slot not in (3, 5) or x % 2 == far:
                    pass_on(slot, x, step)

    flow(7, 1)

    for copy in rest[:3]:
        copy.wait()
    lse_wide[...] = jnp.zeros_like(lse_wide)
    lse_wide[:, 0:TOK] = lse_in[...]
    norms = lse_wide[...] * LOG2E
    rows = lax.broadcasted_iota(jnp.int32, norms.shape, 0)
    lanes = lax.broadcasted_iota(jnp.int32, norms.shape, 1)
    for late in range(2):
        picked = jnp.zeros_like(norms)
        for h in range(GROUP):
            moved = norms
            shift = (h - late) * HALF % HD
            if shift:
                moved = pltpu.roll(norms, shift, 1)
            here = (rows % GROUP == h) & (lanes // HALF == h)
            picked = jnp.where(here, moved, picked)
        total = picked
        for h in range(1, GROUP):
            total = total + pltpu.roll(picked, HQ - h, 0)
        for g in range(HK):
            row = g % HEADS * 2 + late
            aux_send[g // HEADS, row:row + 1, :] = total[GROUP * g:GROUP * g + 1, :]
    ones = jnp.ones((8, HD), BF16)
    for g in range(HK):
        blocks = []
        for late in range(2):
            for h in range(GROUP):
                part = (slice(late * HALF, (late + 1) * HALF),
                        slice((g * GROUP + h) * HD, (g * GROUP + h + 1) * HD))
                blocks.append(do_in[part].astype(F32) * o_in[part].astype(F32))
        product = jnp.concatenate(blocks, axis=0)
        high = product.astype(BF16)
        low = (product - high.astype(F32)).astype(BF16)
        sums = dot(ones, high, ((1,), (1,))) + dot(ones, low, ((1,), (1,)))
        for late in range(2):
            row = 4 + g % HEADS * 2 + late
            aux_send[g // HEADS, row:row + 1, :] = sums[0:1, late * HD:(late + 1) * HD]
    aux[0] = aux_send[me]
    for x in (2, 3, 1):
        remote(aux_send.at[me ^ x], aux.at[x], AUX, aux_r.at[0], at_plane(x)).start()

    flow(6, 2)
    flow(5, 3, (0, 1))

    pltpu.make_async_copy(qd.at[:, 0], qd.at[:, 0], local_sem.at[4]).wait()
    pltpu.make_async_copy(kv.at[0, 0], kv.at[0, 0], local_sem.at[0]).wait()
    all_of(qd.at[:, 1:NI], QD, rows_r.at[0]).wait_recv()
    all_of(aux.at[1:NI], AUX, aux_r.at[0]).wait_recv()
    for x in range(NI):
        stats[:, x * HD:(x + 1) * HD] = aux[x]
        for h in range(HEADS):
            for late in range(2):
                for g in range(GROUP):
                    to = slice((x * GROUP + g) * HALF, (x * GROUP + g + 1) * HALF)
                    tok = slice(late * HALF, (late + 1) * HALF)
                    col = slice((h * GROUP + g) * HD, (h * GROUP + g + 1) * HD)
                    q_rows[h, late, to, :] = qd[0, x, tok, col]
                    do_rows[h, late, to, :] = qd[1, x, tok, col]
    dq_t[...] = jnp.zeros_like(dq_t)

    key_row = lax.broadcasted_iota(jnp.int32, (KEYS, 1), 0)
    key_device = (me ^ (key_row // HALF)) * NZ
    q_lane = lax.broadcasted_iota(jnp.int32, (1, ROWS), 1)
    q_at = ((me ^ (q_lane // (GROUP * HALF))) * NZ + z) * HALF

    def tile(h, late, keys, values, keys_t, key_at):
        q_part = q_rows[h, late]
        do_part = do_rows[h, late]
        row = h * 2 + late
        norm = stats[row:row + 1, :]
        delta = stats[row + 4:row + 5, :]
        scores = dot(keys, q_part, ((1,), (1,)))
        weights = jnp.exp2(scores * (SCALE * LOG2E) - norm)
        sign = -1 if late else 1
        allowed = key_at + key_row % HALF <= sign * q_at + q_lane % HALF
        masked = jnp.where(allowed, weights[-KEYS:], 0.0)
        weights = jnp.concatenate([weights[:-KEYS], masked], axis=0) if late else masked
        dv_add = dot(weights.astype(BF16), do_part, ((1,), (0,)))
        dweights = dot(values, do_part, ((1,), (1,)))
        dscores = (weights * (dweights - delta) * SCALE).astype(BF16)
        dk_add = dot(dscores, q_part, ((1,), (0,)))
        dq_t[h, late] += dot(keys_t, dscores, ((1,), (0,)))
        return dk_add, dv_add

    def unit(slot, h):
        key_z = lax.rem(z + slot, NZ)
        at = (key_device + key_z) * HALF
        early, late = (
            [kv[slot, :, n, part * HALF:(part + 1) * HALF, h * HD:(h + 1) * HD].reshape(KEYS, HD)
             for n in range(2)]
            for part in range(2)
        )
        keys = jnp.concatenate([early[0], late[0]], axis=0)
        values = jnp.concatenate([early[1], late[1]], axis=0)
        keys_t = keys.T
        first = tile(h, 1, keys, values, keys_t, -at)
        second = tile(h, 0, early[0], early[1], keys_t[:, 0:KEYS], at)
        for n in range(2):
            own[slot, h, n, 0:KEYS] = first[n][0:KEYS] + second[n]
            own[slot, h, n, KEYS:] = first[n][KEYS:]

    def hand_back(slot, h, first):
        step = DOWN if slot > 4 or (slot == 4 and h == 0) else UP
        to = (slot - step) % NZ
        if not first:
            all_of(part_recv.at[h, slot], PART, part_r.at[h, slot]).wait_recv()
        for n in range(2):
            total = own[slot, h, n]
            if not first:
                total = total + part_recv[h, slot, n].astype(F32)
            if to:
                part_send[h, slot, n] = total.astype(BF16)
            else:
                stage_last(max(step, 0), h, n, total)
        if to:
            remote(part_send.at[h, slot], part_recv.at[h, to], PART, part_r.at[h, to],
                   at_ring(step)).start()
        else:
            for x in (2, 3, 1, 0):
                send_last(max(step, 0), h, x, dict(at_ring(step), **at_plane(x)))

    def stage_last(way, h, n, total):
        low = total.astype(BF16)
        for x in range(NI):
            for late in range(2):
                last_stage[way, x, h, n, late * HALF:(late + 1) * HALF, :] = (
                    low[(late * NI + x) * HALF:(late * NI + x + 1) * HALF])

    def send_last(way, h, x, where):
        src, dst = last_stage.at[way, x, h], sums_out.at[way, :, :, h_cols(me, h)]
        if way == 2 and x == 0:
            pltpu.make_async_copy(src, dst, local_sem.at[6]).start()
        else:
            remote(src, dst, LAST.at[way // 2], last_r.at[way // 2], where).start()

    def finish_rows(h, late):
        back = dq_t[h, late].T.astype(BF16)
        for x in range(NI):
            for g in range(GROUP):
                dq_stage[x, late * HALF:(late + 1) * HALF,
                         (h * GROUP + g) * HD:(h * GROUP + g + 1) * HD] = (
                    back[(x * GROUP + g) * HALF:(x * GROUP + g + 1) * HALF])

    flow(5, 3, (2,))
    unit(0, 0)
    flow(5, 3, (3,))
    unit(0, 1)
    unit(7, 0)
    for slot, h in ((3, 0), (5, 1)):
        unit(slot, h)
        hand_back(slot, h, True)
    unit(1, 1)
    for h in range(HEADS):
        for n in range(2):
            stage_last(2, h, n, own[0, h, n])
        for x in (2, 3, 1, 0):
            send_last(2, h, x, at_plane(x))
    for x in range(NI):
        arrived(4, x)
    for h in range(HEADS):
        unit(4, h)
        hand_back(4, h, True)
    for slot, h in ((2, 0), (6, 1), (5, 0), (3, 1), (1, 0), (7, 1)):
        unit(slot, h)
        hand_back(slot, h, False)
    unit(6, 0)
    hand_back(6, 0, False)
    finish_rows(0, 0)
    unit(2, 1)
    hand_back(2, 1, False)
    finish_rows(0, 1)
    finish_rows(1, 0)
    finish_rows(1, 1)
    for x in (2, 3, 1):
        remote(dq_stage.at[x], dq_out.at[:, q_cols(me)], DQ, dq_r.at[0], at_plane(x)).start()
    dq_mine = pltpu.make_async_copy(dq_stage.at[0], dq_out.at[:, q_cols(me)], local_sem.at[5])
    dq_mine.start()
    for slot, h in ((7, 0), (1, 1)):
        hand_back(slot, h, False)
    all_of(kv.at[0, 1:NI], PLANE, plane_r.at[0]).wait_send()
    all_of(kv.at[1:NZ], RING, ring_r.at[0, 0]).wait_send()
    all_of(qd.at[:, 1:NI], QD, rows_r.at[0]).wait_send()
    all_of(aux.at[1:NI], AUX, aux_r.at[0]).wait_send()
    all_of(part_send.at[:, 2:NZ - 1], PART, part_r.at[0, 0]).wait_send()
    dq_mine.wait()
    all_of(dq_stage.at[1:NI], DQ, dq_r.at[0]).wait()
    pltpu.make_async_copy(last_stage.at[2, 0], last_stage.at[2, 0], local_sem.at[6]).wait()
    all_of(last_stage.at[2, 1:NI], LAST.at[1], last_r.at[1]).wait()
    all_of(last_stage.at[0:2], LAST.at[0], last_r.at[0]).wait()


def hand_on(dq_ref, sums_ref, dq_out, dk_out, dv_out, total, sems):
    copies = [pltpu.make_async_copy(dq_ref, dq_out, sems.at[0])]
    copies[0].start()
    for n, out in enumerate((dk_out, dv_out)):
        whole = sums_ref[0, n].astype(F32) + sums_ref[1, n].astype(F32) + sums_ref[2, n].astype(F32)
        total[n] = whole.astype(BF16)
        copies.append(pltpu.make_async_copy(total.at[n], out, sems.at[n + 1]))
        copies[-1].start()
    for copy in copies:
        copy.wait()


def on_device(queries, key_rows, value_rows, outputs, out_grads, log_norms):
    dma = pltpu.SemaphoreType.DMA
    operands = (queries, key_rows, value_rows, outputs, out_grads, log_norms)
    operands = tuple(pltpu.with_memory_space_constraint(x, pltpu.HBM) for x in operands)
    grads = pl.pallas_call(
        kernel,
        out_shape=(
            jax.ShapeDtypeStruct((TOK, HQ * HD), BF16),
            jax.ShapeDtypeStruct((3, 2, TOK, HK * HD), BF16),
        ),
        in_specs=[pl.BlockSpec(memory_space=pltpu.HBM)] * 6,
        out_specs=(pl.BlockSpec(memory_space=pl.ANY),) * 2,
        scratch_shapes=[
            pltpu.VMEM((TOK, HQ * HD), BF16),
            pltpu.VMEM((TOK, HQ * HD), BF16),
            pltpu.VMEM((HQ, TOK), F32),
            pltpu.VMEM((HQ, HD), F32),
            pltpu.VMEM((NI, 8, HD), F32),
            pltpu.VMEM((NI, 8, HD), F32),
            pltpu.VMEM((8, ROWS), F32),
            pltpu.VMEM((NZ, NI, 2, TOK, HEADS * HD), BF16),
            pltpu.VMEM((2, NI, TOK, QCOLS), BF16),
            pltpu.VMEM((HEADS, 2, ROWS, HD), BF16),
            pltpu.VMEM((HEADS, 2, ROWS, HD), BF16),
            pltpu.VMEM((HEADS, 2, HD, ROWS), F32),
            pltpu.VMEM((NI, TOK, QCOLS), BF16),
            pltpu.VMEM((NZ, HEADS, 2, 2 * KEYS, HD), F32),
            pltpu.VMEM((HEADS, NZ, 2, 2 * KEYS, HD), BF16),
            pltpu.VMEM((HEADS, NZ, 2, 2 * KEYS, HD), BF16),
            pltpu.VMEM((3, NI, HEADS, 2, TOK, HD), BF16),
            dma((7,)), dma((8,)),
            dma((NI - 1,)), dma((NZ - 1, NI)), dma((HEADS, NZ)),
            dma((1,)), dma((1,)), dma((1,)), dma((2,)),
        ],
        compiler_params=pltpu.CompilerParams(
            collective_id=0, has_side_effects=True, vmem_limit_bytes=40 << 20
        ),
    )(*operands)
    grads = tuple(pltpu.with_memory_space_constraint(g, pltpu.VMEM) for g in grads)
    return pl.pallas_call(
        hand_on,
        out_shape=(
            jax.ShapeDtypeStruct((TOK, HQ * HD), BF16),
            jax.ShapeDtypeStruct((TOK, HK * HD), BF16),
            jax.ShapeDtypeStruct((TOK, HK * HD), BF16),
        ),
        in_specs=[pl.BlockSpec(memory_space=pltpu.VMEM)] * 2,
        out_specs=(pl.BlockSpec(memory_space=pl.ANY),) * 3,
        scratch_shapes=[pltpu.VMEM((2, TOK, HK * HD), BF16), dma((3,))],
    )(*grads)


def solution(mesh):
    rows = P(("head", "inner", "outer"), None)
    return jax.shard_map(
        on_device,
        mesh=mesh,
        in_specs=(rows,) * 5 + (P(None, ("head", "inner", "outer")),),
        out_specs=(rows,) * 3,
        check_vma=False,
    )
```

```python
import jax
import jax.numpy as jnp
from jax import lax
from jax.experimental import pallas as pl
from jax.experimental.pallas import tpu as pltpu
from jax.sharding import PartitionSpec as P

HQ = 32
HK = 8
HD = 128
GROUP = HQ // HK
TOK = 64
HALF = TOK // 2
NZ = 8
NI = 4
HEADS = HK // NI
QCOLS = HEADS * GROUP * HD
KEYS = NI * HALF
ROWS = NI * GROUP * HALF
LOG2E = 1.4426950408889634
SCALE = HD ** -0.5
MESH = pl.DeviceIdType.MESH
F32 = jnp.float32
BF16 = jnp.bfloat16
UP, DOWN = 1, -1


def dot(a, b, dims):
    return lax.dot_general(a, b, (dims, ((), ())), preferred_element_type=F32)


def kernel(
    q_hbm, k_hbm, v_hbm, o_hbm, do_hbm, lse_hbm,
    dq_out, sums_out,
    o_in, do_in, lse_in, lse_wide, aux_send, aux, stats, kv, qd,
    q_rows, do_rows, dq_t, dq_stage, own, part_send, part_recv, last_stage,
    local_sem, send_sem, plane_r, ring_r, part_r, rows_r, aux_r, dq_r, last_r,
):
    me = lax.axis_index("inner")
    z = lax.axis_index("outer")

    def at_ring(step):
        return {"outer": lax.rem(z + step + NZ, NZ)}

    def at_plane(x):
        return {"inner": me ^ x}

    def q_cols(index):
        return pl.ds(pl.multiple_of(index * QCOLS, QCOLS), QCOLS)

    def k_cols(index):
        return pl.ds(pl.multiple_of(index * (HEADS * HD), HEADS * HD), HEADS * HD)

    def h_cols(index, head):
        return pl.ds(pl.multiple_of(index * (HEADS * HD) + head * HD, HD), HD)

    def remote(src, dst, send, recv, where):
        return pltpu.make_async_remote_copy(
            src_ref=src, dst_ref=dst, send_sem=send, recv_sem=recv,
            device_id=where, device_id_type=MESH,
        )

    barrier = pltpu.get_barrier_semaphore()
    for step in (UP, DOWN):
        pl.semaphore_signal(barrier, inc=1, device_id=at_ring(step), device_id_type=MESH)
    for x in range(1, NI):
        pl.semaphore_signal(barrier, inc=1, device_id=at_plane(x), device_id_type=MESH)

    mine = [
        pltpu.make_async_copy(ref.at[:, k_cols(me)], kv.at[0, 0, n], local_sem.at[0])
        for n, ref in enumerate((k_hbm, v_hbm))
    ]
    rest = [
        pltpu.make_async_copy(o_hbm, o_in, local_sem.at[1]),
        pltpu.make_async_copy(do_hbm, do_in, local_sem.at[2]),
        pltpu.make_async_copy(lse_hbm, lse_in, local_sem.at[3]),
        pltpu.make_async_copy(q_hbm.at[:, q_cols(me)], qd.at[0, 0], local_sem.at[4]),
        pltpu.make_async_copy(do_hbm.at[:, q_cols(me)], qd.at[1, 0], local_sem.at[4]),
    ]
    for copy in mine + rest:
        copy.start()
    pl.semaphore_wait(barrier, 2 + NI - 1)

    def all_of(ref, send, recv):
        return remote(ref, ref, send, recv, at_plane(1))

    PLANE, RING, QD, AUX, PART, DQ = (send_sem.at[n] for n in range(6))
    LAST = send_sem.at[6:8]

    def share(x):
        for n, ref in enumerate((k_hbm, v_hbm)):
            remote(ref.at[:, k_cols(me ^ x)], kv.at[0, x, n], PLANE, plane_r.at[x - 1],
                   at_plane(x)).start()

    def pass_first(x, n, step):
        to = -step % NZ
        src = (k_hbm, v_hbm)[n].at[:, k_cols(me)] if x == 0 else kv.at[0, x, n]
        remote(src, kv.at[to, x, n], RING, ring_r.at[to - 1, x], at_ring(step)).start()

    def pass_on(slot, x, step):
        to = (slot - step) % NZ
        remote(kv.at[slot, x], kv.at[to, x], RING, ring_r.at[to - 1, x], at_ring(step)).start()

    def arrived(slot, x):
        all_of(kv.at[slot, x], RING, ring_r.at[slot - 1, x]).wait_recv()

    share(2)
    for n in range(2):
        pass_first(0, n, UP)
        pass_first(0, n, DOWN)
    share(1)
    share(3)
    for x in (1, 2, 3):
        for n, ref in enumerate((q_hbm, do_hbm)):
            remote(ref.at[:, q_cols(me ^ x)], qd.at[n, x], QD, rows_r.at[x // 2], at_plane(x)).start()
    for x in (1, 2, 3):
        all_of(kv.at[0, x], PLANE, plane_r.at[x - 1]).wait_recv()
        for n in range(2):
            pass_first(x, n, UP)
            pass_first(x, n, DOWN)

    def flow(up_slot, down_slot, pieces=range(NI)):
        for x in pieces:
            for slot, step, far in ((up_slot, UP, 0), (down_slot, DOWN, 1)):
                arrived(slot, x)
                if slot not in (3, 5) or x % 2 == far:
                    pass_on(slot, x, step)

    flow(7, 1)

    for copy in rest[:3]:
        copy.wait()
    lse_wide[...] = jnp.zeros_like(lse_wide)
    lse_wide[:, 0:TOK] = lse_in[...]
    norms = lse_wide[...] * LOG2E
    rows = lax.broadcasted_iota(jnp.int32, norms.shape, 0)
    lanes = lax.broadcasted_iota(jnp.int32, norms.shape, 1)
    for late in range(2):
        picked = jnp.zeros_like(norms)
        for h in range(GROUP):
            moved = norms
            shift = (h - late) * HALF % HD
            if shift:
                moved = pltpu.roll(norms, shift, 1)
            here = (rows % GROUP == h) & (lanes // HALF == h)
            picked = jnp.where(here, moved, picked)
        total = picked
        for h in range(1, GROUP):
            total = total + pltpu.roll(picked, HQ - h, 0)
        for g in range(HK):
            row = g % HEADS * 2 + late
            aux_send[g // HEADS, row:row + 1, :] = total[GROUP * g:GROUP * g + 1, :]
    ones = jnp.ones((8, HD), BF16)
    for g in range(HK):
        blocks = []
        for late in range(2):
            for h in range(GROUP):
                part = (slice(late * HALF, (late + 1) * HALF),
                        slice((g * GROUP + h) * HD, (g * GROUP + h + 1) * HD))
                blocks.append(do_in[part].astype(F32) * o_in[part].astype(F32))
        product = jnp.concatenate(blocks, axis=0)
        high = product.astype(BF16)
        low = (product - high.astype(F32)).astype(BF16)
        sums = dot(ones, high, ((1,), (1,))) + dot(ones, low, ((1,), (1,)))
        for late in range(2):
            row = 4 + g % HEADS * 2 + late
            aux_send[g // HEADS, row:row + 1, :] = sums[0:1, late * HD:(late + 1) * HD]
    aux[0] = aux_send[me]
    for x in (2, 3, 1):
        remote(aux_send.at[me ^ x], aux.at[x], AUX, aux_r.at[x // 2], at_plane(x)).start()

    def rows_of(first):
        if first == 0:
            pltpu.make_async_copy(qd.at[:, 0], qd.at[:, 0], local_sem.at[4]).wait()
            pltpu.make_async_copy(kv.at[0, 0], kv.at[0, 0], local_sem.at[0]).wait()
        came = slice(max(first, 1), first + 2)
        all_of(qd.at[:, came], QD, rows_r.at[first // 2]).wait_recv()
        all_of(aux.at[came], AUX, aux_r.at[first // 2]).wait_recv()
        for x in range(first, first + 2):
            stats[:, x * HD:(x + 1) * HD] = aux[x]
            for h in range(HEADS):
                for late in range(2):
                    for g in range(GROUP):
                        to = slice((x * GROUP + g) * HALF, (x * GROUP + g + 1) * HALF)
                        tok = slice(late * HALF, (late + 1) * HALF)
                        col = slice((h * GROUP + g) * HD, (h * GROUP + g + 1) * HD)
                        q_rows[h, late, to, :] = qd[0, x, tok, col]
                        do_rows[h, late, to, :] = qd[1, x, tok, col]

    dq_t[...] = jnp.zeros_like(dq_t)

    key_row = lax.broadcasted_iota(jnp.int32, (KEYS, 1), 0)
    key_device = (me ^ (key_row // HALF)) * NZ
    q_lane = lax.broadcasted_iota(jnp.int32, (1, ROWS), 1)
    q_at = ((me ^ (q_lane // (GROUP * HALF))) * NZ + z) * HALF

    def tile(h, late, keys, values, keys_t, key_at, span):
        q_part = q_rows[h, late, span]
        do_part = do_rows[h, late, span]
        row = h * 2 + late
        norm = stats[row:row + 1, span]
        delta = stats[row + 4:row + 5, span]
        scores = dot(keys, q_part, ((1,), (1,)))
        weights = jnp.exp2(scores * (SCALE * LOG2E) - norm)
        sign = -1 if late else 1
        allowed = key_at + key_row % HALF <= (sign * q_at + q_lane % HALF)[:, span]
        masked = jnp.where(allowed, weights[-KEYS:], 0.0)
        weights = jnp.concatenate([weights[:-KEYS], masked], axis=0) if late else masked
        dv_add = dot(weights.astype(BF16), do_part, ((1,), (0,)))
        dweights = dot(values, do_part, ((1,), (1,)))
        dscores = (weights * (dweights - delta) * SCALE).astype(BF16)
        dk_add = dot(dscores, q_part, ((1,), (0,)))
        dq_t[h, late, :, span] += dot(keys_t, dscores, ((1,), (0,)))
        return dk_add, dv_add

    def unit(slot, h, part=None):
        span = slice(0, ROWS) if part is None else slice(part * ROWS // 2, (part + 1) * ROWS // 2)
        key_z = lax.rem(z + slot, NZ)
        at = (key_device + key_z) * HALF
        early, late = (
            [kv[slot, :, n, part * HALF:(part + 1) * HALF, h * HD:(h + 1) * HD].reshape(KEYS, HD)
             for n in range(2)]
            for part in range(2)
        )
        keys = jnp.concatenate([early[0], late[0]], axis=0)
        values = jnp.concatenate([early[1], late[1]], axis=0)
        keys_t = keys.T
        first = tile(h, 1, keys, values, keys_t, -at, span)
        second = tile(h, 0, early[0], early[1], keys_t[:, 0:KEYS], at, span)
        for n in range(2):
            if part == 1:
                own[slot, h, n, 0:KEYS] += first[n][0:KEYS] + second[n]
                own[slot, h, n, KEYS:] += first[n][KEYS:]
            else:
                own[slot, h, n, 0:KEYS] = first[n][0:KEYS] + second[n]
                own[slot, h, n, KEYS:] = first[n][KEYS:]

    def hand_back(slot, h, first):
        step = DOWN if slot > 4 or (slot == 4 and h == 0) else UP
        to = (slot - step) % NZ
        if not first:
            all_of(part_recv.at[h, slot], PART, part_r.at[h, slot]).wait_recv()
        for n in range(2):
            total = own[slot, h, n]
            if not first:
                total = total + part_recv[h, slot, n].astype(F32)
            if to:
                part_send[h, slot, n] = total.astype(BF16)
            else:
                stage_last(max(step, 0), h, n, total)
        if to:
            remote(part_send.at[h, slot], part_recv.at[h, to], PART, part_r.at[h, to],
                   at_ring(step)).start()
        else:
            for x in (2, 3, 1, 0):
                send_last(max(step, 0), h, x, dict(at_ring(step), **at_plane(x)))

    def stage_last(way, h, n, total):
        low = total.astype(BF16)
        for x in range(NI):
            for late in range(2):
                last_stage[way, x, h, n, late * HALF:(late + 1) * HALF, :] = (
                    low[(late * NI + x) * HALF:(late * NI + x + 1) * HALF])

    def send_last(way, h, x, where):
        src, dst = last_stage.at[way, x, h], sums_out.at[way, :, :, h_cols(me, h)]
        if way == 2 and x == 0:
            pltpu.make_async_copy(src, dst, local_sem.at[6]).start()
        else:
            remote(src, dst, LAST.at[way // 2], last_r.at[way // 2], where).start()

    def finish_rows(h):
        for late in range(2):
            back = dq_t[h, late].T.astype(BF16)
            for x in range(NI):
                for g in range(GROUP):
                    dq_stage[h, x, late * HALF:(late + 1) * HALF, g * HD:(g + 1) * HD] = (
                        back[(x * GROUP + g) * HALF:(x * GROUP + g + 1) * HALF])
        cols = pl.ds(pl.multiple_of((me * HEADS + h) * GROUP * HD, GROUP * HD), GROUP * HD)
        for x in (2, 3, 1):
            remote(dq_stage.at[h, x], dq_out.at[:, cols], DQ, dq_r.at[0], at_plane(x)).start()
        pltpu.make_async_copy(dq_stage.at[h, 0], dq_out.at[:, cols], local_sem.at[5]).start()

    rows_of(0)
    for x, units in enumerate((((0, 0),), ((0, 1),), ((7, 0),), ((1, 1),))):
        flow(6, 2, (x,))
        for slot, h in units:
            unit(slot, h, 0)
    unit(7, 1, 0)
    unit(1, 0, 0)
    for x, units in enumerate((((6, 0), (2, 1)), ((6, 1), (2, 0)))):
        flow(5, 3, (x,))
        for slot, h in units:
            unit(slot, h, 0)
    rows_of(2)
    flow(5, 3, (2,))
    unit(0, 0, 1)
    flow(5, 3, (3,))
    unit(0, 1, 1)
    for slot, h in ((3, 0), (5, 1)):
        unit(slot, h)
        hand_back(slot, h, True)
    for slot, h in ((7, 0), (1, 1)):
        unit(slot, h, 1)
    for h in range(HEADS):
        for n in range(2):
            stage_last(2, h, n, own[0, h, n])
        for x in (2, 3, 1, 0):
            send_last(2, h, x, at_plane(x))
    for x in range(NI):
        arrived(4, x)
    for h in range(HEADS):
        unit(4, h)
        hand_back(4, h, True)
    for slot, h in ((2, 0), (6, 1)):
        unit(slot, h, 1)
        hand_back(slot, h, False)
    unit(5, 0)
    unit(3, 1)
    hand_back(5, 0, False)
    hand_back(3, 1, False)
    unit(1, 0, 1)
    unit(6, 0, 1)
    hand_back(1, 0, False)
    finish_rows(0)
    unit(7, 1, 1)
    hand_back(7, 1, False)
    hand_back(6, 0, False)
    unit(2, 1, 1)
    hand_back(2, 1, False)
    finish_rows(1)
    for slot, h in ((7, 0), (1, 1)):
        hand_back(slot, h, False)

    all_of(kv.at[0, 1:NI], PLANE, plane_r.at[0]).wait_send()
    all_of(kv.at[1:NZ], RING, ring_r.at[0, 0]).wait_send()
    all_of(qd.at[:, 1:NI], QD, rows_r.at[0]).wait_send()
    all_of(aux.at[1:NI], AUX, aux_r.at[0]).wait_send()
    all_of(part_send.at[:, 2:NZ - 1], PART, part_r.at[0, 0]).wait_send()
    pltpu.make_async_copy(dq_stage.at[:, 0], dq_stage.at[:, 0], local_sem.at[5]).wait()
    all_of(dq_stage.at[:, 1:NI], DQ, dq_r.at[0]).wait()
    pltpu.make_async_copy(last_stage.at[2, 0], last_stage.at[2, 0], local_sem.at[6]).wait()
    all_of(last_stage.at[2, 1:NI], LAST.at[1], last_r.at[1]).wait()
    all_of(last_stage.at[0:2], LAST.at[0], last_r.at[0]).wait()


def hand_on(dq_ref, sums_ref, dq_out, dk_out, dv_out, total, sems):
    copies = [pltpu.make_async_copy(dq_ref, dq_out, sems.at[0])]
    copies[0].start()
    for n, out in enumerate((dk_out, dv_out)):
        whole = sums_ref[0, n].astype(F32) + sums_ref[1, n].astype(F32) + sums_ref[2, n].astype(F32)
        total[n] = whole.astype(BF16)
        copies.append(pltpu.make_async_copy(total.at[n], out, sems.at[n + 1]))
        copies[-1].start()
    for copy in copies:
        copy.wait()


def on_device(queries, key_rows, value_rows, outputs, out_grads, log_norms):
    dma = pltpu.SemaphoreType.DMA
    operands = (queries, key_rows, value_rows, outputs, out_grads, log_norms)
    operands = tuple(pltpu.with_memory_space_constraint(x, pltpu.HBM) for x in operands)
    grads = pl.pallas_call(
        kernel,
        out_shape=(
            jax.ShapeDtypeStruct((TOK, HQ * HD), BF16),
            jax.ShapeDtypeStruct((3, 2, TOK, HK * HD), BF16),
        ),
        in_specs=[pl.BlockSpec(memory_space=pltpu.HBM)] * 6,
        out_specs=(pl.BlockSpec(memory_space=pl.ANY),) * 2,
        scratch_shapes=[
            pltpu.VMEM((TOK, HQ * HD), BF16),
            pltpu.VMEM((TOK, HQ * HD), BF16),
            pltpu.VMEM((HQ, TOK), F32),
            pltpu.VMEM((HQ, HD), F32),
            pltpu.VMEM((NI, 8, HD), F32),
            pltpu.VMEM((NI, 8, HD), F32),
            pltpu.VMEM((8, ROWS), F32),
            pltpu.VMEM((NZ, NI, 2, TOK, HEADS * HD), BF16),
            pltpu.VMEM((2, NI, TOK, QCOLS), BF16),
            pltpu.VMEM((HEADS, 2, ROWS, HD), BF16),
            pltpu.VMEM((HEADS, 2, ROWS, HD), BF16),
            pltpu.VMEM((HEADS, 2, HD, ROWS), F32),
            pltpu.VMEM((HEADS, NI, TOK, GROUP * HD), BF16),
            pltpu.VMEM((NZ, HEADS, 2, 2 * KEYS, HD), F32),
            pltpu.VMEM((HEADS, NZ, 2, 2 * KEYS, HD), BF16),
            pltpu.VMEM((HEADS, NZ, 2, 2 * KEYS, HD), BF16),
            pltpu.VMEM((3, NI, HEADS, 2, TOK, HD), BF16),
            dma((7,)), dma((8,)),
            dma((NI - 1,)), dma((NZ - 1, NI)), dma((HEADS, NZ)),
            dma((2,)), dma((2,)), dma((1,)), dma((2,)),
        ],
        compiler_params=pltpu.CompilerParams(
            collective_id=0, has_side_effects=True, vmem_limit_bytes=40 << 20
        ),
    )(*operands)
    grads = tuple(pltpu.with_memory_space_constraint(g, pltpu.VMEM) for g in grads)
    return pl.pallas_call(
        hand_on,
        out_shape=(
            jax.ShapeDtypeStruct((TOK, HQ * HD), BF16),
            jax.ShapeDtypeStruct((TOK, HK * HD), BF16),
            jax.ShapeDtypeStruct((TOK, HK * HD), BF16),
        ),
        in_specs=[pl.BlockSpec(memory_space=pltpu.VMEM)] * 2,
        out_specs=(pl.BlockSpec(memory_space=pl.ANY),) * 3,
        scratch_shapes=[pltpu.VMEM((2, TOK, HK * HD), BF16), dma((3,))],
    )(*grads)


def solution(mesh):
    rows = P(("head", "inner", "outer"), None)
    return jax.shard_map(
        on_device,
        mesh=mesh,
        in_specs=(rows,) * 5 + (P(None, ("head", "inner", "outer")),),
        out_specs=(rows,) * 3,
        check_vma=False,
    )
```

```python
import jax
import jax.numpy as jnp
from jax import lax
from jax.experimental import pallas as pl
from jax.experimental.pallas import tpu as pltpu
from jax.sharding import PartitionSpec as P

HQ = 32
HK = 8
HD = 128
GROUP = HQ // HK
TOK = 64
HALF = TOK // 2
NZ = 8
NI = 4
HEADS = HK // NI
QCOLS = HEADS * GROUP * HD
KEYS = NI * HALF
ROWS = NI * GROUP * HALF
LOG2E = 1.4426950408889634
SCALE = HD ** -0.5
MESH = pl.DeviceIdType.MESH
F32 = jnp.float32
BF16 = jnp.bfloat16
UP, DOWN = 1, -1


def dot(a, b, dims):
    return lax.dot_general(a, b, (dims, ((), ())), preferred_element_type=F32)


def kernel(
    q_hbm, k_hbm, v_hbm, o_hbm, do_hbm, lse_hbm,
    dq_out, sums_out,
    o_in, do_in, lse_in, lse_wide, aux_send, aux, stats, kv, qd,
    q_rows, do_rows, dq_t, dq_stage, own, part_send, part_recv, last_stage,
    local_sem, send_sem, plane_r, ring_r, part_r, rows_r, aux_r, dq_r, last_r,
):
    me = lax.axis_index("inner")
    z = lax.axis_index("outer")

    def at_ring(step):
        return {"outer": lax.rem(z + step + NZ, NZ)}

    def at_plane(x):
        return {"inner": me ^ x}

    def q_cols(index):
        return pl.ds(pl.multiple_of(index * QCOLS, QCOLS), QCOLS)

    def k_cols(index):
        return pl.ds(pl.multiple_of(index * (HEADS * HD), HEADS * HD), HEADS * HD)

    def h_cols(index, head):
        return pl.ds(pl.multiple_of(index * (HEADS * HD) + head * HD, HD), HD)

    def remote(src, dst, send, recv, where):
        return pltpu.make_async_remote_copy(
            src_ref=src, dst_ref=dst, send_sem=send, recv_sem=recv,
            device_id=where, device_id_type=MESH,
        )

    barrier = pltpu.get_barrier_semaphore()
    for step in (UP, DOWN):
        pl.semaphore_signal(barrier, inc=1, device_id=at_ring(step), device_id_type=MESH)
    for x in range(1, NI):
        pl.semaphore_signal(barrier, inc=1, device_id=at_plane(x), device_id_type=MESH)

    mine = [
        pltpu.make_async_copy(ref.at[:, k_cols(me)], kv.at[0, 0, n], local_sem.at[0])
        for n, ref in enumerate((k_hbm, v_hbm))
    ]
    rest = [
        pltpu.make_async_copy(o_hbm, o_in, local_sem.at[1]),
        pltpu.make_async_copy(do_hbm, do_in, local_sem.at[2]),
        pltpu.make_async_copy(lse_hbm, lse_in, local_sem.at[3]),
        pltpu.make_async_copy(q_hbm.at[:, q_cols(me)], qd.at[0, 0], local_sem.at[4]),
        pltpu.make_async_copy(do_hbm.at[:, q_cols(me)], qd.at[1, 0], local_sem.at[4]),
    ]
    pl.semaphore_wait(barrier, 2 + NI - 1)

    def all_of(ref, send, recv):
        return remote(ref, ref, send, recv, at_plane(1))

    PLANE, RING, QD, AUX, PART, DQ = (send_sem.at[n] for n in range(6))
    LAST = send_sem.at[6:8]

    def share(x):
        for n, ref in enumerate((k_hbm, v_hbm)):
            remote(ref.at[:, k_cols(me ^ x)], kv.at[0, x, n], PLANE, plane_r.at[x - 1],
                   at_plane(x)).start()

    def pass_first(x, n, step):
        to = -step % NZ
        src = (k_hbm, v_hbm)[n].at[:, k_cols(me)] if x == 0 else kv.at[0, x, n]
        remote(src, kv.at[to, x, n], RING, ring_r.at[to - 1, x], at_ring(step)).start()

    def pass_on(slot, x, step):
        to = (slot - step) % NZ
        remote(kv.at[slot, x], kv.at[to, x], RING, ring_r.at[to - 1, x], at_ring(step)).start()

    def arrived(slot, x):
        all_of(kv.at[slot, x], RING, ring_r.at[slot - 1, x]).wait_recv()

    share(2)
    for n in range(2):
        pass_first(0, n, UP)
        pass_first(0, n, DOWN)
    share(1)
    share(3)
    for copy in mine + rest:
        copy.start()
    for x in (1, 2, 3):
        for n, ref in enumerate((q_hbm, do_hbm)):
            remote(ref.at[:, q_cols(me ^ x)], qd.at[n, x], QD, rows_r.at[x // 2], at_plane(x)).start()
    for x in (1, 2, 3):
        all_of(kv.at[0, x], PLANE, plane_r.at[x - 1]).wait_recv()
        for n in range(2):
            pass_first(x, n, UP)
            pass_first(x, n, DOWN)

    def flow(up_slot, down_slot, pieces=range(NI)):
        for x in pieces:
            for slot, step, far in ((up_slot, UP, 0), (down_slot, DOWN, 1)):
                arrived(slot, x)
                if slot not in (3, 5) or x % 2 == far:
                    pass_on(slot, x, step)

    flow(7, 1)

    for copy in rest[:3]:
        copy.wait()
    lse_wide[...] = jnp.zeros_like(lse_wide)
    lse_wide[:, 0:TOK] = lse_in[...]
    norms = lse_wide[...] * LOG2E
    rows = lax.broadcasted_iota(jnp.int32, norms.shape, 0)
    lanes = lax.broadcasted_iota(jnp.int32, norms.shape, 1)
    for late in range(2):
        picked = jnp.zeros_like(norms)
        for h in range(GROUP):
            moved = norms
            shift = (h - late) * HALF % HD
            if shift:
                moved = pltpu.roll(norms, shift, 1)
            here = (rows % GROUP == h) & (lanes // HALF == h)
            picked = jnp.where(here, moved, picked)
        total = picked
        for h in range(1, GROUP):
            total = total + pltpu.roll(picked, HQ - h, 0)
        for g in range(HK):
            row = g % HEADS * 2 + late
            aux_send[g // HEADS, row:row + 1, :] = total[GROUP * g:GROUP * g + 1, :]
    ones = jnp.ones((8, HD), BF16)
    for g in range(HK):
        blocks = []
        for late in range(2):
            for h in range(GROUP):
                part = (slice(late * HALF, (late + 1) * HALF),
                        slice((g * GROUP + h) * HD, (g * GROUP + h + 1) * HD))
                blocks.append(do_in[part].astype(F32) * o_in[part].astype(F32))
        product = jnp.concatenate(blocks, axis=0)
        high = product.astype(BF16)
        low = (product - high.astype(F32)).astype(BF16)
        sums = dot(ones, high, ((1,), (1,))) + dot(ones, low, ((1,), (1,)))
        for late in range(2):
            row = 4 + g % HEADS * 2 + late
            aux_send[g // HEADS, row:row + 1, :] = sums[0:1, late * HD:(late + 1) * HD]
    aux[0] = aux_send[me]
    for x in (2, 3, 1):
        remote(aux_send.at[me ^ x], aux.at[x], AUX, aux_r.at[x // 2], at_plane(x)).start()

    def rows_of(first):
        if first == 0:
            pltpu.make_async_copy(qd.at[:, 0], qd.at[:, 0], local_sem.at[4]).wait()
            pltpu.make_async_copy(kv.at[0, 0], kv.at[0, 0], local_sem.at[0]).wait()
        came = slice(max(first, 1), first + 2)
        all_of(qd.at[:, came], QD, rows_r.at[first // 2]).wait_recv()
        all_of(aux.at[came], AUX, aux_r.at[first // 2]).wait_recv()
        for x in range(first, first + 2):
            stats[:, x * HD:(x + 1) * HD] = aux[x]
            for h in range(HEADS):
                for late in range(2):
                    for g in range(GROUP):
                        to = slice((x * GROUP + g) * HALF, (x * GROUP + g + 1) * HALF)
                        tok = slice(late * HALF, (late + 1) * HALF)
                        col = slice((h * GROUP + g) * HD, (h * GROUP + g + 1) * HD)
                        q_rows[h, late, to, :] = qd[0, x, tok, col]
                        do_rows[h, late, to, :] = qd[1, x, tok, col]

    dq_t[...] = jnp.zeros_like(dq_t)

    key_row = lax.broadcasted_iota(jnp.int32, (KEYS, 1), 0)
    key_device = (me ^ (key_row // HALF)) * NZ
    q_lane = lax.broadcasted_iota(jnp.int32, (1, ROWS), 1)
    q_at = ((me ^ (q_lane // (GROUP * HALF))) * NZ + z) * HALF

    def tile(h, late, keys, values, keys_t, key_at, span):
        q_part = q_rows[h, late, span]
        do_part = do_rows[h, late, span]
        scores = dot(keys, q_part, ((1,), (1,)))
        dweights = dot(values, do_part, ((1,), (1,)))

        def finish():
            row = h * 2 + late
            norm = stats[row:row + 1, span]
            delta = stats[row + 4:row + 5, span]
            weights = jnp.exp2(scores * (SCALE * LOG2E) - norm)
            sign = -1 if late else 1
            allowed = key_at + key_row % HALF <= (sign * q_at + q_lane % HALF)[:, span]
            masked = jnp.where(allowed, weights[-KEYS:], 0.0)
            full = jnp.concatenate([weights[:-KEYS], masked], axis=0) if late else masked
            dscores = (full * (dweights - delta) * SCALE).astype(BF16)
            dv_add = dot(full.astype(BF16), do_part, ((1,), (0,)))
            dk_add = dot(dscores, q_part, ((1,), (0,)))
            dq_t[h, late, :, span] += dot(keys_t, dscores, ((1,), (0,)))
            return dk_add, dv_add

        return finish

    def unit(slot, h, part=None):
        span = slice(0, ROWS) if part is None else slice(part * ROWS // 2, (part + 1) * ROWS // 2)
        key_z = lax.rem(z + slot, NZ)
        at = (key_device + key_z) * HALF
        early, late = (
            [kv[slot, :, n, part * HALF:(part + 1) * HALF, h * HD:(h + 1) * HD].reshape(KEYS, HD)
             for n in range(2)]
            for part in range(2)
        )
        keys = jnp.concatenate([early[0], late[0]], axis=0)
        values = jnp.concatenate([early[1], late[1]], axis=0)
        keys_t = keys.T
        first = tile(h, 1, keys, values, keys_t, -at, span)
        second = tile(h, 0, early[0], early[1], keys_t[:, 0:KEYS], at, span)
        first, second = first(), second()
        for n in range(2):
            if part == 1:
                own[slot, h, n, 0:KEYS] += first[n][0:KEYS] + second[n]
                own[slot, h, n, KEYS:] += first[n][KEYS:]
            else:
                own[slot, h, n, 0:KEYS] = first[n][0:KEYS] + second[n]
                own[slot, h, n, KEYS:] = first[n][KEYS:]

    def hand_back(slot, h, first):
        step = DOWN if slot > 4 or (slot == 4 and h == 0) else UP
        to = (slot - step) % NZ
        if not first:
            all_of(part_recv.at[h, slot], PART, part_r.at[h, slot]).wait_recv()
        for n in range(2):
            total = own[slot, h, n]
            if not first:
                total = total + part_recv[h, slot, n].astype(F32)
            if to:
                part_send[h, slot, n] = total.astype(BF16)
            else:
                stage_last(max(step, 0), h, n, total)
        if to:
            remote(part_send.at[h, slot], part_recv.at[h, to], PART, part_r.at[h, to],
                   at_ring(step)).start()
        else:
            for x in (2, 3, 1, 0):
                send_last(max(step, 0), h, x, dict(at_ring(step), **at_plane(x)))

    def stage_last(way, h, n, total):
        low = total.astype(BF16)
        for x in range(NI):
            for late in range(2):
                last_stage[way, x, h, n, late * HALF:(late + 1) * HALF, :] = (
                    low[(late * NI + x) * HALF:(late * NI + x + 1) * HALF])

    def send_last(way, h, x, where):
        src, dst = last_stage.at[way, x, h], sums_out.at[way, :, :, h_cols(me, h)]
        if way == 2 and x == 0:
            pltpu.make_async_copy(src, dst, local_sem.at[6]).start()
        else:
            remote(src, dst, LAST.at[way // 2], last_r.at[way // 2], where).start()

    def finish_rows(h):
        for late in range(2):
            back = dq_t[h, late].T.astype(BF16)
            for x in range(NI):
                for g in range(GROUP):
                    dq_stage[h, x, late * HALF:(late + 1) * HALF, g * HD:(g + 1) * HD] = (
                        back[(x * GROUP + g) * HALF:(x * GROUP + g + 1) * HALF])
        cols = pl.ds(pl.multiple_of((me * HEADS + h) * GROUP * HD, GROUP * HD), GROUP * HD)
        for x in (2, 3, 1):
            remote(dq_stage.at[h, x], dq_out.at[:, cols], DQ, dq_r.at[0], at_plane(x)).start()
        pltpu.make_async_copy(dq_stage.at[h, 0], dq_out.at[:, cols], local_sem.at[5]).start()

    rows_of(0)
    for x, units in enumerate((((0, 0),), ((0, 1),), ((7, 0),), ((1, 1),))):
        flow(6, 2, (x,))
        for slot, h in units:
            unit(slot, h, 0)
    unit(7, 1, 0)
    unit(1, 0, 0)
    for x, units in enumerate((((6, 0), (2, 1)), ((6, 1), (2, 0)))):
        flow(5, 3, (x,))
        for slot, h in units:
            unit(slot, h, 0)
    rows_of(2)
    flow(5, 3, (2,))
    unit(0, 0, 1)
    flow(5, 3, (3,))
    for slot, h in ((3, 0), (5, 1)):
        unit(slot, h)
        hand_back(slot, h, True)
    unit(0, 1, 1)
    for x in range(NI):
        arrived(4, x)
    for h in range(HEADS):
        unit(4, h)
        hand_back(4, h, True)
    for slot, h in ((2, 0), (6, 1)):
        unit(slot, h, 1)
        hand_back(slot, h, False)
    unit(5, 0)
    unit(3, 1)
    hand_back(5, 0, False)
    hand_back(3, 1, False)
    for h in range(HEADS):
        for n in range(2):
            stage_last(2, h, n, own[0, h, n])
        for x in (2, 3, 1, 0):
            send_last(2, h, x, at_plane(x))
    unit(7, 0, 1)
    unit(1, 0, 1)
    unit(6, 0, 1)
    hand_back(1, 0, False)
    finish_rows(0)
    unit(7, 1, 1)
    hand_back(7, 1, False)
    hand_back(6, 0, False)
    unit(1, 1, 1)
    unit(2, 1, 1)
    hand_back(2, 1, False)
    finish_rows(1)
    for slot, h in ((7, 0), (1, 1)):
        hand_back(slot, h, False)

    all_of(kv.at[0, 1:NI], PLANE, plane_r.at[0]).wait_send()
    all_of(kv.at[1:NZ], RING, ring_r.at[0, 0]).wait_send()
    all_of(qd.at[:, 1:NI], QD, rows_r.at[0]).wait_send()
    all_of(aux.at[1:NI], AUX, aux_r.at[0]).wait_send()
    all_of(part_send.at[:, 2:NZ - 1], PART, part_r.at[0, 0]).wait_send()
    pltpu.make_async_copy(dq_stage.at[:, 0], dq_stage.at[:, 0], local_sem.at[5]).wait()
    all_of(dq_stage.at[:, 1:NI], DQ, dq_r.at[0]).wait()
    pltpu.make_async_copy(last_stage.at[2, 0], last_stage.at[2, 0], local_sem.at[6]).wait()
    all_of(last_stage.at[2, 1:NI], LAST.at[1], last_r.at[1]).wait()
    all_of(last_stage.at[0:2], LAST.at[0], last_r.at[0]).wait()


def hand_on(dq_ref, sums_ref, dq_out, dk_out, dv_out, total, sems):
    copies = [pltpu.make_async_copy(dq_ref, dq_out, sems.at[0])]
    copies[0].start()
    for n, out in enumerate((dk_out, dv_out)):
        whole = sums_ref[0, n].astype(F32) + sums_ref[1, n].astype(F32) + sums_ref[2, n].astype(F32)
        total[n] = whole.astype(BF16)
        copies.append(pltpu.make_async_copy(total.at[n], out, sems.at[n + 1]))
        copies[-1].start()
    for copy in copies:
        copy.wait()


def on_device(queries, key_rows, value_rows, outputs, out_grads, log_norms):
    dma = pltpu.SemaphoreType.DMA
    operands = (queries, key_rows, value_rows, outputs, out_grads, log_norms)
    operands = tuple(pltpu.with_memory_space_constraint(x, pltpu.HBM) for x in operands)
    grads = pl.pallas_call(
        kernel,
        out_shape=(
            jax.ShapeDtypeStruct((TOK, HQ * HD), BF16),
            jax.ShapeDtypeStruct((3, 2, TOK, HK * HD), BF16),
        ),
        in_specs=[pl.BlockSpec(memory_space=pltpu.HBM)] * 6,
        out_specs=(pl.BlockSpec(memory_space=pl.ANY),) * 2,
        scratch_shapes=[
            pltpu.VMEM((TOK, HQ * HD), BF16),
            pltpu.VMEM((TOK, HQ * HD), BF16),
            pltpu.VMEM((HQ, TOK), F32),
            pltpu.VMEM((HQ, HD), F32),
            pltpu.VMEM((NI, 8, HD), F32),
            pltpu.VMEM((NI, 8, HD), F32),
            pltpu.VMEM((8, ROWS), F32),
            pltpu.VMEM((NZ, NI, 2, TOK, HEADS * HD), BF16),
            pltpu.VMEM((2, NI, TOK, QCOLS), BF16),
            pltpu.VMEM((HEADS, 2, ROWS, HD), BF16),
            pltpu.VMEM((HEADS, 2, ROWS, HD), BF16),
            pltpu.VMEM((HEADS, 2, HD, ROWS), F32),
            pltpu.VMEM((HEADS, NI, TOK, GROUP * HD), BF16),
            pltpu.VMEM((NZ, HEADS, 2, 2 * KEYS, HD), F32),
            pltpu.VMEM((HEADS, NZ, 2, 2 * KEYS, HD), BF16),
            pltpu.VMEM((HEADS, NZ, 2, 2 * KEYS, HD), BF16),
            pltpu.VMEM((3, NI, HEADS, 2, TOK, HD), BF16),
            dma((7,)), dma((8,)),
            dma((NI - 1,)), dma((NZ - 1, NI)), dma((HEADS, NZ)),
            dma((2,)), dma((2,)), dma((1,)), dma((2,)),
        ],
        compiler_params=pltpu.CompilerParams(
            collective_id=0, has_side_effects=True, vmem_limit_bytes=40 << 20
        ),
    )(*operands)
    grads = tuple(pltpu.with_memory_space_constraint(g, pltpu.VMEM) for g in grads)
    return pl.pallas_call(
        hand_on,
        out_shape=(
            jax.ShapeDtypeStruct((TOK, HQ * HD), BF16),
            jax.ShapeDtypeStruct((TOK, HK * HD), BF16),
            jax.ShapeDtypeStruct((TOK, HK * HD), BF16),
        ),
        in_specs=[pl.BlockSpec(memory_space=pltpu.VMEM)] * 2,
        out_specs=(pl.BlockSpec(memory_space=pl.ANY),) * 3,
        scratch_shapes=[pltpu.VMEM((2, TOK, HK * HD), BF16), dma((3,))],
    )(*grads)


def solution(mesh):
    rows = P(("head", "inner", "outer"), None)
    return jax.shard_map(
        on_device,
        mesh=mesh,
        in_specs=(rows,) * 5 + (P(None, ("head", "inner", "outer")),),
        out_specs=(rows,) * 3,
        check_vma=False,
    )
```

```python
import jax
import jax.numpy as jnp
from jax import lax
from jax.experimental import pallas as pl
from jax.experimental.pallas import tpu as pltpu
from jax.sharding import PartitionSpec as P

HQ = 32
HK = 8
HD = 128
GROUP = HQ // HK
TOK = 64
HALF = TOK // 2
NZ = 8
NI = 4
HEADS = HK // NI
QCOLS = HEADS * GROUP * HD
KEYS = NI * HALF
ROWS = NI * GROUP * HALF
LOG2E = 1.4426950408889634
SCALE = HD ** -0.5
MESH = pl.DeviceIdType.MESH
F32 = jnp.float32
BF16 = jnp.bfloat16
UP, DOWN = 1, -1


def dot(a, b, dims):
    return lax.dot_general(a, b, (dims, ((), ())), preferred_element_type=F32)


def kernel(
    q_hbm, k_hbm, v_hbm, o_hbm, do_hbm, lse_hbm,
    dq_out, sums_out,
    o_in, do_in, lse_in, lse_wide, aux_send, aux, stats, kv, qd,
    q_rows, do_rows, dq_t, dq_stage, own, part_send, part_recv, last_stage,
    local_sem, send_sem, plane_r, ring_r, part_r, rows_r, aux_r, dq_r, last_r,
):
    me = lax.axis_index("inner")
    z = lax.axis_index("outer")

    def at_ring(step):
        return {"outer": lax.rem(z + step + NZ, NZ)}

    def at_plane(x):
        return {"inner": me ^ x}

    def q_cols(index):
        return pl.ds(pl.multiple_of(index * QCOLS, QCOLS), QCOLS)

    def k_cols(index):
        return pl.ds(pl.multiple_of(index * (HEADS * HD), HEADS * HD), HEADS * HD)

    def h_cols(index, head):
        return pl.ds(pl.multiple_of(index * (HEADS * HD) + head * HD, HD), HD)

    def remote(src, dst, send, recv, where):
        return pltpu.make_async_remote_copy(
            src_ref=src, dst_ref=dst, send_sem=send, recv_sem=recv,
            device_id=where, device_id_type=MESH,
        )

    barrier = pltpu.get_barrier_semaphore()
    for step in (UP, DOWN):
        pl.semaphore_signal(barrier, inc=1, device_id=at_ring(step), device_id_type=MESH)
    for x in range(1, NI):
        pl.semaphore_signal(barrier, inc=1, device_id=at_plane(x), device_id_type=MESH)

    mine = [
        pltpu.make_async_copy(ref.at[:, k_cols(me)], kv.at[0, 0, n], local_sem.at[0])
        for n, ref in enumerate((k_hbm, v_hbm))
    ]
    rest = [
        pltpu.make_async_copy(o_hbm, o_in, local_sem.at[1]),
        pltpu.make_async_copy(do_hbm, do_in, local_sem.at[2]),
        pltpu.make_async_copy(lse_hbm, lse_in, local_sem.at[3]),
        pltpu.make_async_copy(q_hbm.at[:, q_cols(me)], qd.at[0, 0], local_sem.at[4]),
        pltpu.make_async_copy(do_hbm.at[:, q_cols(me)], qd.at[1, 0], local_sem.at[4]),
    ]
    pl.semaphore_wait(barrier, 2 + NI - 1)

    def all_of(ref, send, recv):
        return remote(ref, ref, send, recv, at_plane(1))

    PLANE, RING, QD, AUX, PART, DQ = (send_sem.at[n] for n in range(6))
    LAST = send_sem.at[6:8]

    def share(x):
        for n, ref in enumerate((k_hbm, v_hbm)):
            remote(ref.at[:, k_cols(me ^ x)], kv.at[0, x, n], PLANE, plane_r.at[x - 1],
                   at_plane(x)).start()

    def pass_first(x, n, step):
        to = -step % NZ
        src = (k_hbm, v_hbm)[n].at[:, k_cols(me)] if x == 0 else kv.at[0, x, n]
        remote(src, kv.at[to, x, n], RING, ring_r.at[to - 1, x], at_ring(step)).start()

    def pass_on(slot, x, step):
        to = (slot - step) % NZ
        remote(kv.at[slot, x], kv.at[to, x], RING, ring_r.at[to - 1, x], at_ring(step)).start()

    def arrived(slot, x):
        all_of(kv.at[slot, x], RING, ring_r.at[slot - 1, x]).wait_recv()

    share(2)
    for n in range(2):
        pass_first(0, n, UP)
        pass_first(0, n, DOWN)
    share(1)
    share(3)
    for copy in mine + rest:
        copy.start()
    for x in (1, 2, 3):
        for n, ref in enumerate((q_hbm, do_hbm)):
            remote(ref.at[:, q_cols(me ^ x)], qd.at[n, x], QD, rows_r.at[x // 2], at_plane(x)).start()
    for x in (1, 2, 3):
        all_of(kv.at[0, x], PLANE, plane_r.at[x - 1]).wait_recv()
        pass_on(0, x, UP)
        pass_on(0, x, DOWN)

    def flow(up_slot, down_slot, pieces=range(NI)):
        for x in pieces:
            for slot, step, far in ((up_slot, UP, 0), (down_slot, DOWN, 1)):
                arrived(slot, x)
                if slot not in (3, 5) or x % 2 == far:
                    pass_on(slot, x, step)

    flow(7, 1)

    for copy in rest[:3]:
        copy.wait()
    lse_wide[...] = jnp.zeros_like(lse_wide)
    lse_wide[:, 0:TOK] = lse_in[...]
    norms = lse_wide[...] * LOG2E
    rows = lax.broadcasted_iota(jnp.int32, norms.shape, 0)
    lanes = lax.broadcasted_iota(jnp.int32, norms.shape, 1)
    for late in range(2):
        picked = jnp.zeros_like(norms)
        for h in range(GROUP):
            moved = norms
            shift = (h - late) * HALF % HD
            if shift:
                moved = pltpu.roll(norms, shift, 1)
            here = (rows % GROUP == h) & (lanes // HALF == h)
            picked = jnp.where(here, moved, picked)
        total = picked
        for h in range(1, GROUP):
            total = total + pltpu.roll(picked, HQ - h, 0)
        for g in range(HK):
            row = g % HEADS * 2 + late
            aux_send[g // HEADS, row:row + 1, :] = total[GROUP * g:GROUP * g + 1, :]
    ones = jnp.ones((8, HD), BF16)
    for g in range(HK):
        blocks = []
        for late in range(2):
            for h in range(GROUP):
                part = (slice(late * HALF, (late + 1) * HALF),
                        slice((g * GROUP + h) * HD, (g * GROUP + h + 1) * HD))
                blocks.append(do_in[part].astype(F32) * o_in[part].astype(F32))
        product = jnp.concatenate(blocks, axis=0)
        high = product.astype(BF16)
        low = (product - high.astype(F32)).astype(BF16)
        sums = dot(ones, high, ((1,), (1,))) + dot(ones, low, ((1,), (1,)))
        for late in range(2):
            row = 4 + g % HEADS * 2 + late
            aux_send[g // HEADS, row:row + 1, :] = sums[0:1, late * HD:(late + 1) * HD]
    aux[0] = aux_send[me]
    for x in (2, 3, 1):
        remote(aux_send.at[me ^ x], aux.at[x], AUX, aux_r.at[x // 2], at_plane(x)).start()

    def rows_of(first):
        if first == 0:
            pltpu.make_async_copy(qd.at[:, 0], qd.at[:, 0], local_sem.at[4]).wait()
            pltpu.make_async_copy(kv.at[0, 0], kv.at[0, 0], local_sem.at[0]).wait()
        came = slice(max(first, 1), first + 2)
        all_of(qd.at[:, came], QD, rows_r.at[first // 2]).wait_recv()
        all_of(aux.at[came], AUX, aux_r.at[first // 2]).wait_recv()
        for x in range(first, first + 2):
            stats[:, x * HD:(x + 1) * HD] = aux[x]
            for h in range(HEADS):
                for late in range(2):
                    for g in range(GROUP):
                        to = slice((x * GROUP + g) * HALF, (x * GROUP + g + 1) * HALF)
                        tok = slice(late * HALF, (late + 1) * HALF)
                        col = slice((h * GROUP + g) * HD, (h * GROUP + g + 1) * HD)
                        q_rows[h, late, to, :] = qd[0, x, tok, col]
                        do_rows[h, late, to, :] = qd[1, x, tok, col]

    dq_t[...] = jnp.zeros_like(dq_t)

    key_row = lax.broadcasted_iota(jnp.int32, (KEYS, 1), 0)
    key_device = (me ^ (key_row // HALF)) * NZ
    q_lane = lax.broadcasted_iota(jnp.int32, (1, ROWS), 1)
    q_at = ((me ^ (q_lane // (GROUP * HALF))) * NZ + z) * HALF

    def tile(h, late, keys, values, keys_t, key_at, span):
        q_part = q_rows[h, late, span]
        do_part = do_rows[h, late, span]
        scores = dot(keys, q_part, ((1,), (1,)))
        dweights = dot(values, do_part, ((1,), (1,)))

        def finish():
            row = h * 2 + late
            norm = stats[row:row + 1, span]
            delta = stats[row + 4:row + 5, span]
            weights = jnp.exp2(scores * (SCALE * LOG2E) - norm)
            sign = -1 if late else 1
            allowed = key_at + key_row % HALF <= (sign * q_at + q_lane % HALF)[:, span]
            masked = jnp.where(allowed, weights[-KEYS:], 0.0)
            full = jnp.concatenate([weights[:-KEYS], masked], axis=0) if late else masked
            dscores = (full * (dweights - delta) * SCALE).astype(BF16)
            dv_add = dot(full.astype(BF16), do_part, ((1,), (0,)))
            dk_add = dot(dscores, q_part, ((1,), (0,)))
            dq_t[h, late, :, span] += dot(keys_t, dscores, ((1,), (0,)))
            return dk_add, dv_add

        return finish

    def unit(slot, h, part=None):
        span = slice(0, ROWS) if part is None else slice(part * ROWS // 2, (part + 1) * ROWS // 2)
        key_z = lax.rem(z + slot, NZ)
        at = (key_device + key_z) * HALF
        early, late = (
            [kv[slot, :, n, part * HALF:(part + 1) * HALF, h * HD:(h + 1) * HD].reshape(KEYS, HD)
             for n in range(2)]
            for part in range(2)
        )
        keys = jnp.concatenate([early[0], late[0]], axis=0)
        values = jnp.concatenate([early[1], late[1]], axis=0)
        keys_t = keys.T
        first = tile(h, 1, keys, values, keys_t, -at, span)
        second = tile(h, 0, early[0], early[1], keys_t[:, 0:KEYS], at, span)
        first, second = first(), second()
        for n in range(2):
            if part == 1:
                own[slot, h, n, 0:KEYS] += first[n][0:KEYS] + second[n]
                own[slot, h, n, KEYS:] += first[n][KEYS:]
            else:
                own[slot, h, n, 0:KEYS] = first[n][0:KEYS] + second[n]
                own[slot, h, n, KEYS:] = first[n][KEYS:]

    def hand_back(slot, h, first):
        step = DOWN if slot > 4 or (slot == 4 and h == 0) else UP
        to = (slot - step) % NZ
        if not first:
            all_of(part_recv.at[h, slot], PART, part_r.at[h, slot]).wait_recv()
        for n in range(2):
            total = own[slot, h, n]
            if not first:
                total = total + part_recv[h, slot, n].astype(F32)
            if to:
                part_send[h, slot, n] = total.astype(BF16)
            else:
                stage_last(max(step, 0), h, n, total)
        if to:
            remote(part_send.at[h, slot], part_recv.at[h, to], PART, part_r.at[h, to],
                   at_ring(step)).start()
        else:
            for x in (2, 3, 1, 0):
                send_last(max(step, 0), h, x, dict(at_ring(step), **at_plane(x)))

    def stage_last(way, h, n, total):
        low = total.astype(BF16)
        for x in range(NI):
            for late in range(2):
                last_stage[way, x, h, n, late * HALF:(late + 1) * HALF, :] = (
                    low[(late * NI + x) * HALF:(late * NI + x + 1) * HALF])

    def send_last(way, h, x, where):
        src, dst = last_stage.at[way, x, h], sums_out.at[way, :, :, h_cols(me, h)]
        if way == 2 and x == 0:
            pltpu.make_async_copy(src, dst, local_sem.at[6]).start()
        else:
            remote(src, dst, LAST.at[way // 2], last_r.at[way // 2], where).start()

    def finish_rows(h):
        for late in range(2):
            back = dq_t[h, late].T.astype(BF16)
            for x in range(NI):
                for g in range(GROUP):
                    dq_stage[h, x, late * HALF:(late + 1) * HALF, g * HD:(g + 1) * HD] = (
                        back[(x * GROUP + g) * HALF:(x * GROUP + g + 1) * HALF])
        cols = pl.ds(pl.multiple_of((me * HEADS + h) * GROUP * HD, GROUP * HD), GROUP * HD)
        for x in (2, 3, 1):
            remote(dq_stage.at[h, x], dq_out.at[:, cols], DQ, dq_r.at[0], at_plane(x)).start()
        pltpu.make_async_copy(dq_stage.at[h, 0], dq_out.at[:, cols], local_sem.at[5]).start()

    rows_of(0)
    for x, units in enumerate((((0, 0),), ((0, 1),), ((7, 0),), ((1, 1),))):
        flow(6, 2, (x,))
        for slot, h in units:
            unit(slot, h, 0)
    unit(7, 1, 0)
    unit(1, 0, 0)
    for x, units in enumerate((((6, 0), (2, 1)), ((6, 1), (2, 0)))):
        flow(5, 3, (x,))
        for slot, h in units:
            unit(slot, h, 0)
    rows_of(2)
    flow(5, 3, (2,))
    unit(0, 0, 1)
    flow(5, 3, (3,))
    for slot, h in ((3, 0), (5, 1)):
        unit(slot, h)
        hand_back(slot, h, True)
    unit(0, 1, 1)
    for x in range(NI):
        arrived(4, x)
    for h in range(HEADS):
        unit(4, h)
        hand_back(4, h, True)
    for slot, h in ((2, 0), (6, 1)):
        unit(slot, h, 1)
        hand_back(slot, h, False)
    unit(5, 0)
    unit(3, 1)
    hand_back(5, 0, False)
    hand_back(3, 1, False)
    for h in range(HEADS):
        for n in range(2):
            stage_last(2, h, n, own[0, h, n])
        for x in (2, 3, 1, 0):
            send_last(2, h, x, at_plane(x))
    unit(7, 0, 1)
    unit(1, 0, 1)
    unit(6, 0, 1)
    hand_back(1, 0, False)
    finish_rows(0)
    unit(7, 1, 1)
    hand_back(7, 1, False)
    hand_back(6, 0, False)
    unit(1, 1, 1)
    unit(2, 1, 1)
    hand_back(2, 1, False)
    finish_rows(1)
    for slot, h in ((7, 0), (1, 1)):
        hand_back(slot, h, False)

    all_of(kv.at[0, 1:NI], PLANE, plane_r.at[0]).wait_send()
    all_of(kv.at[1:NZ], RING, ring_r.at[0, 0]).wait_send()
    all_of(qd.at[:, 1:NI], QD, rows_r.at[0]).wait_send()
    all_of(aux.at[1:NI], AUX, aux_r.at[0]).wait_send()
    all_of(part_send.at[:, 2:NZ - 1], PART, part_r.at[0, 0]).wait_send()
    pltpu.make_async_copy(dq_stage.at[:, 0], dq_stage.at[:, 0], local_sem.at[5]).wait()
    all_of(dq_stage.at[:, 1:NI], DQ, dq_r.at[0]).wait()
    pltpu.make_async_copy(last_stage.at[2, 0], last_stage.at[2, 0], local_sem.at[6]).wait()
    all_of(last_stage.at[2, 1:NI], LAST.at[1], last_r.at[1]).wait()
    all_of(last_stage.at[0:2], LAST.at[0], last_r.at[0]).wait()


def hand_on(dq_ref, sums_ref, dq_out, dk_out, dv_out, total, sems):
    copies = [pltpu.make_async_copy(dq_ref, dq_out, sems.at[0])]
    copies[0].start()
    for n, out in enumerate((dk_out, dv_out)):
        whole = sums_ref[0, n].astype(F32) + sums_ref[1, n].astype(F32) + sums_ref[2, n].astype(F32)
        total[n] = whole.astype(BF16)
        copies.append(pltpu.make_async_copy(total.at[n], out, sems.at[n + 1]))
        copies[-1].start()
    for copy in copies:
        copy.wait()


def on_device(queries, key_rows, value_rows, outputs, out_grads, log_norms):
    dma = pltpu.SemaphoreType.DMA
    operands = (queries, key_rows, value_rows, outputs, out_grads, log_norms)
    operands = tuple(pltpu.with_memory_space_constraint(x, pltpu.HBM) for x in operands)
    grads = pl.pallas_call(
        kernel,
        out_shape=(
            jax.ShapeDtypeStruct((TOK, HQ * HD), BF16),
            jax.ShapeDtypeStruct((3, 2, TOK, HK * HD), BF16),
        ),
        in_specs=[pl.BlockSpec(memory_space=pltpu.HBM)] * 6,
        out_specs=(pl.BlockSpec(memory_space=pl.ANY),) * 2,
        scratch_shapes=[
            pltpu.VMEM((TOK, HQ * HD), BF16),
            pltpu.VMEM((TOK, HQ * HD), BF16),
            pltpu.VMEM((HQ, TOK), F32),
            pltpu.VMEM((HQ, HD), F32),
            pltpu.VMEM((NI, 8, HD), F32),
            pltpu.VMEM((NI, 8, HD), F32),
            pltpu.VMEM((8, ROWS), F32),
            pltpu.VMEM((NZ, NI, 2, TOK, HEADS * HD), BF16),
            pltpu.VMEM((2, NI, TOK, QCOLS), BF16),
            pltpu.VMEM((HEADS, 2, ROWS, HD), BF16),
            pltpu.VMEM((HEADS, 2, ROWS, HD), BF16),
            pltpu.VMEM((HEADS, 2, HD, ROWS), F32),
            pltpu.VMEM((HEADS, NI, TOK, GROUP * HD), BF16),
            pltpu.VMEM((NZ, HEADS, 2, 2 * KEYS, HD), F32),
            pltpu.VMEM((HEADS, NZ, 2, 2 * KEYS, HD), BF16),
            pltpu.VMEM((HEADS, NZ, 2, 2 * KEYS, HD), BF16),
            pltpu.VMEM((3, NI, HEADS, 2, TOK, HD), BF16),
            dma((7,)), dma((8,)),
            dma((NI - 1,)), dma((NZ - 1, NI)), dma((HEADS, NZ)),
            dma((2,)), dma((2,)), dma((1,)), dma((2,)),
        ],
        compiler_params=pltpu.CompilerParams(
            collective_id=0, has_side_effects=True, vmem_limit_bytes=40 << 20
        ),
    )(*operands)
    grads = tuple(pltpu.with_memory_space_constraint(g, pltpu.VMEM) for g in grads)
    return pl.pallas_call(
        hand_on,
        out_shape=(
            jax.ShapeDtypeStruct((TOK, HQ * HD), BF16),
            jax.ShapeDtypeStruct((TOK, HK * HD), BF16),
            jax.ShapeDtypeStruct((TOK, HK * HD), BF16),
        ),
        in_specs=[pl.BlockSpec(memory_space=pltpu.VMEM)] * 2,
        out_specs=(pl.BlockSpec(memory_space=pl.ANY),) * 3,
        scratch_shapes=[pltpu.VMEM((2, TOK, HK * HD), BF16), dma((3,))],
    )(*grads)


def solution(mesh):
    rows = P(("head", "inner", "outer"), None)
    return jax.shard_map(
        on_device,
        mesh=mesh,
        in_specs=(rows,) * 5 + (P(None, ("head", "inner", "outer")),),
        out_specs=(rows,) * 3,
        check_vma=False,
    )
```
